512 devices in a mesh: slab: 16 (over x_lo, z), sub: 32 (over y, x_hi, core).
Axes of the slice: x: 4 (x_hi: 2, x_lo: 2; x = x_hi * 2 + x_lo), y: 8, z: 8, core: 2. Of those that a mesh axis runs over, the one named last changes fastest.
Arguments:
- positions: float32 [3, 131072], P(None, ('slab', 'sub')), may hold values from 0 to 1
- features: bfloat16 [64, 131072], P(None, ('slab', 'sub')), may hold values from -6 to 6
- neighbours: int32 [16, 131072], P(None, ('slab', 'sub')), may hold values from 0 to 383
- miller: int32 [3, 2048], replicated, may hold values from -4 to 4
- filter_weights: float32 [2048, 64], replicated, may hold values from -6 to 6
- energy_weights: float32 [64], replicated, may hold values from -0.06 to 0.06
Outputs:
- updated: float32 [64, 131072], P(None, ('slab', 'sub'))
- forces: float32 [3, 131072], P(None, ('slab', 'sub'))
The draws below stay inside these ranges and needn't reach their ends.
Inputs may be any that keep to these rules, and one draw needn't show every extreme that they name: `neighbours`: an index below 64 names a row of the lower neighbouring slab's block, an index of 320 or more one of the upper slab's block, the others the block's own atoms, as in the reference program.
All inputs are finite; a program needn't handle non-finite values.
Results may differ from the reference program's by a relative error of at most 0.0005.
Values sent between devices are 32-bit elements; how exact they have to be, the bound alone decides.
A program may use at most 64 MiB of HBM per device.

```python
import math
import jax
import jax.numpy as jnp
from jax import lax

ATOM_DEV = 256
GHOST = 64
NBR = 16
KVEC = 2048
CHANNELS = 64
ATOMS = 131072
N_SLAB = 16
N_SUB = 32


def with_ends(array, key, low, largest):
    index_at = [jax.random.randint(jax.random.fold_in(key, axis), (), 0, length) for axis, length in enumerate(array.shape)]
    longest = array.shape.index(max(array.shape))
    beside = index_at[:longest] + [(index_at[longest] + 1) % array.shape[longest]] + index_at[longest + 1:]
    return array.at[tuple(index_at)].set(low).at[tuple(beside)].set(largest)


def steps_of(rng, dims, cuts, smallest, high):
    def one(dim, shards_of):
        draws = jax.random.uniform(jax.random.fold_in(jax.random.fold_in(rng, 6), dim), (shards_of,), jnp.float32, smallest / len(cuts), high / len(cuts))
        return jnp.repeat(jnp.exp(draws), dims[dim] // shards_of).reshape((-1,) + (1,) * (len(dims) - dim - 1))

    gain = one(*cuts[0])
    for cut in cuts[1:]:
        gain = gain * one(*cut)
    return gain


def gaussian(own_key, extent, deviation, reach, shards=(), kind=jnp.bfloat16):
    result = deviation * jax.random.normal(own_key, extent, jnp.float32)
    if shards:
        result = result * steps_of(own_key, extent, shards, -0.22, 0.18)
    return jnp.clip(result, -reach, reach).astype(kind)


def setup_inputs(seed: int = 0) -> dict:
    arg_keys = jax.random.split(jax.random.key(seed), 7)
    return {
        "positions": jnp.clip(1.0 * jax.random.uniform(arg_keys[0], (3, ATOMS), jnp.float32) ** steps_of(arg_keys[0], (3, ATOMS), ((1, 512),), -0.2, 0.2), 0.0, 1.0),
        "features": gaussian(arg_keys[1], (CHANNELS, ATOMS), 1.0, 6.0, ((1, 512),)),
        "neighbours": with_ends(jax.random.randint(arg_keys[2], (NBR, ATOMS), 0, ATOM_DEV + 2 * GHOST), jax.random.fold_in(arg_keys[2], 1), 0, (ATOM_DEV + 2 * GHOST) - 1).astype(jnp.int32),
        "miller": with_ends(jax.random.randint(arg_keys[3], (3, KVEC), -4, 5), jax.random.fold_in(arg_keys[3], 1), -4, 4).astype(jnp.int32),
        "filter_weights": gaussian(arg_keys[4], (KVEC, CHANNELS), 1.0, 6.0, (), jnp.float32),
        "energy_weights": gaussian(arg_keys[5], (CHANNELS,), 0.01, 0.06, (), jnp.float32),
    }


TWO_PI = 2.0 * math.pi
BETA = 1.0
SHORT_SCALE = 0.25
KBLOCK = 256

def exact_dot(left, right):
    return jnp.dot(left, right, precision=lax.Precision.HIGHEST, preferred_element_type=jnp.float32)

def phase_pair(positions, miller_block):
    miller_float = miller_block.astype(jnp.float32)
    angle = TWO_PI * (miller_float[0][:, None] * positions[0][None, :] + miller_float[1][:, None] * positions[1][None, :] + miller_float[2][:, None] * positions[2][None, :])
    return (jnp.cos(angle), jnp.sin(angle))

def over_kvec(miller, running, update):
    kvec_total = miller.shape[1]
    block_size = min(KBLOCK, kvec_total)

    def advance(carry, block_index):
        first_k = block_index * block_size
        miller_block = lax.dynamic_slice_in_dim(miller, first_k, block_size, 1)
        return update(carry, miller_block, first_k, block_size)
    return lax.scan(advance, running, jnp.arange(kvec_total // block_size, dtype=jnp.int32))

def factor_part(positions, values, miller):

    def update(carry, miller_block, first_k, block_size):
        cosines, sines = phase_pair(positions, miller_block)
        return (carry, jnp.concatenate([exact_dot(cosines, values.T), exact_dot(sines, values.T)], 1))
    _, stacked = over_kvec(miller, jnp.zeros((), jnp.float32), update)
    return stacked.reshape(miller.shape[1], 2 * values.shape[0])

def long_eval(positions, miller, weighted):
    channels = weighted.shape[1] // 2

    def update(running, miller_block, first_k, block_size):
        cosines, sines = phase_pair(positions, miller_block)
        rows_here = lax.dynamic_slice_in_dim(weighted, first_k, block_size, 0)
        running = running + exact_dot(rows_here[:, :channels].T, cosines) + exact_dot(rows_here[:, channels:].T, sines)
        return (running, jnp.zeros((), jnp.float32))
    final, _ = over_kvec(miller, jnp.zeros((channels, positions.shape[1]), jnp.float32), update)
    return final

def phase_force(positions, miller, weighted, grads, energy_grad, feat_wide):
    channels = weighted.shape[1] // 2
    paired = jnp.concatenate([energy_grad, feat_wide], 0)

    def update(running, miller_block, first_k, block_size):
        cosines, sines = phase_pair(positions, miller_block)
        rows_w = lax.dynamic_slice_in_dim(weighted, first_k, block_size, 0)
        rows_g = lax.dynamic_slice_in_dim(grads, first_k, block_size, 0)
        real_side = exact_dot(jnp.concatenate([rows_w[:, :channels], rows_g[:, :channels]], 1), paired)
        imag_side = exact_dot(jnp.concatenate([rows_w[:, channels:], rows_g[:, channels:]], 1), paired)
        angle_grad = cosines * imag_side - sines * real_side
        running = running + TWO_PI * exact_dot(miller_block.astype(jnp.float32), angle_grad)
        return (running, jnp.zeros((), jnp.float32))
    final, _ = over_kvec(miller, jnp.zeros((3, positions.shape[1]), jnp.float32), update)
    return final

def short_terms(own_pos, ext_pos, ext_feat, neighbours):

    def one_slot(running, index_row):
        near_pos = jnp.take(ext_pos, index_row, axis=1)
        near_feat = jnp.take(ext_feat, index_row, axis=1)
        offset = own_pos - near_pos
        weight = jnp.exp(BETA * (lax.optimization_barrier(jnp.sum(jnp.cos(TWO_PI * offset), 0)) - 3.0))
        return (running + weight[None, :] * near_feat, None)
    empty_sum = jnp.zeros((ext_feat.shape[0], own_pos.shape[1]), jnp.float32)
    summed, _ = lax.scan(one_slot, empty_sum, neighbours)
    return SHORT_SCALE * summed

def short_grad(own_pos, ext_pos, ext_feat, neighbours, energy_grad):

    def one_slot(running, index_row):
        own_acc, ext_acc = running
        near_pos = jnp.take(ext_pos, index_row, axis=1)
        near_feat = jnp.take(ext_feat, index_row, axis=1)
        offset = own_pos - near_pos
        weight = jnp.exp(BETA * (lax.optimization_barrier(jnp.sum(jnp.cos(TWO_PI * offset), 0)) - 3.0))
        weight_grad = SHORT_SCALE * lax.optimization_barrier(jnp.sum(energy_grad * near_feat, 0))
        force_term = (weight_grad * weight * BETA * -TWO_PI)[None, :] * jnp.sin(TWO_PI * offset)
        own_acc = own_acc + force_term
        ext_acc = ext_acc.at[:, index_row].add(-force_term)
        return ((own_acc, ext_acc), None)
    start_own = jnp.zeros((3, own_pos.shape[1]), jnp.float32)
    start_ext = jnp.zeros((3, ext_pos.shape[1]), jnp.float32)
    (own_acc, ext_acc), _ = lax.scan(one_slot, (start_own, start_ext), neighbours)
    return (own_acc, ext_acc)

def to_blocks(values, width):
    rows_count = values.shape[0]
    return jnp.moveaxis(values.reshape(rows_count, N_SLAB * N_SUB, width), 1, 0)

def from_blocks(values):
    return jnp.moveaxis(values, 0, 1).reshape(values.shape[1], -1)

def extend(values):
    rows_count = values.shape[0]
    grid = values.reshape(rows_count, N_SLAB, N_SUB, ATOM_DEV)
    lower_rim = jnp.roll(grid[..., ATOM_DEV - GHOST:], 1, axis=1)
    upper_rim = jnp.roll(grid[..., :GHOST], -1, axis=1)
    joined = jnp.concatenate([lower_rim, grid, upper_rim], -1).reshape(rows_count, -1)
    return to_blocks(joined, ATOM_DEV + 2 * GHOST)

def reference(positions, features, neighbours, miller, filter_weights, energy_weights):
    feat_wide = features.astype(jnp.float32)
    norm_scale = 1.0 / math.sqrt(ATOM_DEV * N_SLAB * N_SUB * KVEC)
    pos_blocks = to_blocks(positions, ATOM_DEV)
    feat_blocks = to_blocks(feat_wide, ATOM_DEV)
    near_blocks = to_blocks(neighbours, ATOM_DEV)

    def accumulate(running, inputs):
        return (running + factor_part(inputs[0], inputs[1], miller), None)
    empty_factor = jnp.zeros((KVEC, 2 * CHANNELS), jnp.float32)
    factor, _ = lax.scan(accumulate, empty_factor, (pos_blocks, feat_blocks))
    filter_pair = jnp.concatenate([filter_weights, filter_weights], 1)
    weighted = norm_scale * filter_pair * factor
    long_part = lax.map(lambda block_pos: long_eval(block_pos, miller, weighted), pos_blocks)
    ext_pos = extend(positions)
    ext_feat = extend(feat_wide)
    short_part = jax.vmap(short_terms)(pos_blocks, ext_pos, ext_feat, near_blocks)
    updated_blocks = feat_blocks + short_part + long_part
    squashed = jnp.tanh(updated_blocks)
    energy_grad = energy_weights[None, :, None] * (1.0 - squashed * squashed)
    grads_sum, _ = lax.scan(accumulate, empty_factor, (pos_blocks, energy_grad))
    grads = norm_scale * filter_pair * grads_sum
    long_grad = lax.map(lambda inputs: phase_force(inputs[0], miller, weighted, grads, inputs[1], inputs[2]), (pos_blocks, energy_grad, feat_blocks))
    own_grads, ext_grads = jax.vmap(short_grad)(pos_blocks, ext_pos, ext_feat, near_blocks, energy_grad)
    own_grads = own_grads + ext_grads[..., GHOST:GHOST + ATOM_DEV]
    lower_back = ext_grads[..., :GHOST].reshape(N_SLAB, N_SUB, 3, GHOST)
    upper_back = ext_grads[..., GHOST + ATOM_DEV:].reshape(N_SLAB, N_SUB, 3, GHOST)
    own_grid = own_grads.reshape(N_SLAB, N_SUB, 3, ATOM_DEV)
    own_grid = own_grid.at[..., ATOM_DEV - GHOST:].add(jnp.roll(lower_back, -1, axis=0))
    own_grid = own_grid.at[..., :GHOST].add(jnp.roll(upper_back, 1, axis=0))
    forces_blocks = -(long_grad + own_grid.reshape(N_SLAB * N_SUB, 3, ATOM_DEV))
    return (from_blocks(updated_blocks), from_blocks(forces_blocks))
```

```python
import functools
import math

import jax
import jax.numpy as jnp
import numpy as np
from jax import lax
from jax.experimental import pallas as pl
from jax.experimental.pallas import tpu as pltpu
from jax.sharding import PartitionSpec as P

F32 = jnp.float32
BF16 = jnp.bfloat16
MESH = pl.DeviceIdType.MESH
TWO_PI = 2.0 * math.pi

NZ, NY, NX, NC = 8, 8, 4, 2
ATOMS_DEV = 256
GHOST = 64
NBR = 16
HALF = 41
GROUP = NZ * NC
WIDE = GROUP * ATOMS_DEV
CHUNK = 1024

RING = sorted(
    [(dz, dc) for dz in range(NZ) for dc in range(NC)],
    key=lambda o: (min(o[0], NZ - o[0]), o[0], o[1]),
)
ARRIVALS = ((0, 2), (2, 6), (6, 10), (10, 14), (14, 16))


def cos_coefficients():
    nodes = np.cos(np.pi * (np.arange(64) + 0.5) / 64)
    square = (nodes + 1) / 8
    fit = np.polynomial.chebyshev.Chebyshev.fit(
        square, np.cos(2 * np.pi * np.sqrt(square)), 7, domain=[0, 0.25]
    )
    return [float(v) for v in fit.convert(kind=np.polynomial.Polynomial).coef]


COS = cos_coefficients()


def cos_turns(turns):
    reduced = turns - jnp.round(turns)
    square = reduced * reduced
    value = jnp.full_like(square, COS[-1])
    for factor in COS[-2::-1]:
        value = value * square + factor
    return value


def halves(value):
    high = value.astype(BF16).astype(F32)
    return high, value - high


def stacked_halves(value):
    return jnp.concatenate(halves(value), 0).astype(BF16)


def dot(left, right, contract=(1, 0)):
    return lax.dot_general(
        left, right, (((contract[0],), (contract[1],)), ((), ())), preferred_element_type=F32
    )


def exact(left, right, contract=(1, 0)):
    return lax.dot_general(
        left,
        right,
        (((contract[0],), (contract[1],)), ((), ())),
        precision=lax.Precision.HIGHEST,
        preferred_element_type=F32,
    )


def rows_like(shape):
    return lax.broadcasted_iota(jnp.int32, shape, 0)


def lanes_like(shape):
    return lax.broadcasted_iota(jnp.int32, shape, 1)


def turn_rows(value):
    return pltpu.roll(value, 4, 0)


def turn_lanes(value, by):
    return pltpu.roll(value, by % 128, 1)


def swap_sides(value):
    lane = lanes_like(value.shape)
    return jnp.where(lane < HALF, turn_lanes(value, -HALF), turn_lanes(value, HALF))


def pack_modes(modes):
    lane = lanes_like((8, 128))
    row = rows_like((8, 128))
    t0, t1, t2, t3, t4 = (modes[8 * i : 8 * i + 8] for i in range(5))
    used = lane < 2 * HALF
    return jnp.concatenate(
        [
            jnp.where(used, t0, turn_lanes(t3, 2 * HALF)),
            jnp.where(used, t1, turn_lanes(t3, HALF)),
            jnp.where(
                used, t2, jnp.where(row < 4, turn_lanes(t4, 2 * HALF), turn_lanes(t4, HALF))
            ),
        ],
        0,
    )


def unpack_modes(packed):
    lane = lanes_like((8, 128))
    row = rows_like((8, 128))
    p0, p1, p2 = (packed[8 * i : 8 * i + 8] for i in range(3))
    used = lane < 2 * HALF
    t0, t1, t2 = (jnp.where(used, p, 0.0) for p in (p0, p1, p2))
    t3 = jnp.where(lane < HALF, turn_lanes(p0, -2 * HALF), turn_lanes(p1, -HALF))
    t4 = jnp.where(lane < HALF, turn_lanes(p2, -2 * HALF), turn_lanes(turn_rows(p2), -HALF))
    t3 = jnp.where(used, t3, 0.0)
    t4 = jnp.where(used & (row < 4), t4, 0.0)
    return t0, t1, t2, t3, t4


def weigh(packed, filters):
    t0, t1, t2, t3, t4 = unpack_modes(packed)
    sum12, sum34, sum0 = filters[0:8], filters[8:16], filters[16:24]
    dif12, dif34 = filters[24:32], filters[32:40]
    return jnp.concatenate(
        [
            sum12 * t0 + dif12 * swap_sides(t2),
            sum34 * t1 + dif34 * swap_sides(t3),
            sum12 * t2 - dif12 * swap_sides(t0),
            sum34 * t3 - dif34 * swap_sides(t1),
            sum0 * t4,
        ],
        0,
    )


def with_slopes(weighted):
    lane = lanes_like(weighted.shape)
    pair = jnp.where(lane < HALF, lane, lane - HALF)
    along_y = (pair + 4) // 9
    along_z = pair - 9 * along_y
    sign = jnp.where(lane < HALF, TWO_PI, -TWO_PI)
    sign = jnp.where(lane < 2 * HALF, sign, 0.0)
    swapped = swap_sides(weighted)
    return jnp.concatenate(
        [
            weighted,
            swapped * (sign * along_y.astype(F32)),
            swapped * (sign * along_z.astype(F32)),
        ],
        0,
    )


def left_operand(modes):
    high, low = halves(modes)
    return jnp.concatenate(
        [
            jnp.concatenate([high, high], 1),
            jnp.concatenate([low, jnp.zeros_like(low)], 1),
        ],
        0,
    ).astype(BF16)


def kernel(
    pos_ref,
    feat_ref,
    near_ref,
    miller_ref,
    filter_ref,
    energy_ref,
    upd_ref,
    force_ref,
    tx1,
    rx1,
    ext,
    basis,
    xbasis,
    feat8,
    grad8,
    slopes,
    pairs,
    y1,
    x1,
    y2,
    x2,
    part1,
    part1x,
    part2,
    part2x,
    tx_short,
    rx_short,
    tx_upd,
    rx_upd,
    tx_force,
    rx_force,
    ghost_out,
    ghost_in,
    first_sem,
    recv_sem,
    send_sem,
):
    slab = lax.axis_index("slab")
    sub = lax.axis_index("sub")
    z = lax.rem(slab, NZ)
    x_lo = slab // NZ
    y = sub // 4
    x_hi = lax.rem(sub // 2, 2)
    core = lax.rem(sub, 2)
    x = x_hi * 2 + x_lo

    def at(zz, cc):
        return {"slab": x_lo * NZ + zz, "sub": y * 4 + x_hi * 2 + cc}

    def ring(off):
        return lax.rem(z + off[0], NZ), lax.rem(core + off[1], NC)

    def ring_back(off):
        return lax.rem(z + NZ - off[0], NZ), lax.rem(core + off[1], NC)

    def along_y(d):
        return {"slab": slab, "sub": lax.rem(y + d, NY) * 4 + x_hi * 2 + core}

    def along_x(d):
        xx = lax.rem(x + d, NX)
        return {"slab": lax.rem(xx, 2) * NZ + z, "sub": y * 4 + (xx // 2) * 2 + core}

    upper = {"slab": lax.rem(slab + 1, 16), "sub": sub}
    lower = {"slab": lax.rem(slab + 15, 16), "sub": sub}

    def send(src, dst, send_at, recv, device):
        pltpu.make_async_remote_copy(
            src_ref=src,
            dst_ref=dst,
            send_sem=send_at,
            recv_sem=recv,
            device_id=device,
            device_id_type=MESH,
        ).start()

    def wait(ref, sem):
        pltpu.make_async_copy(ref, ref, sem).wait()

    barrier = pltpu.get_barrier_semaphore()
    greeted = [at(*ring(off)) for off in RING[:0:-1]]
    greeted += [along_y(d) for d in range(1, NY)]
    greeted += [along_x(d) for d in range(1, NX)]
    greeted += [upper, lower]
    for device in greeted:
        pl.semaphore_signal(barrier, inc=1, device_id=device, device_id_type=MESH)

    row8 = rows_like((8, ATOMS_DEV))
    tile_row = rows_like((8, 128))
    first4 = row8 < 4

    feats = feat_ref[...].astype(F32)
    place = jnp.concatenate([pos_ref[...], jnp.zeros((5, ATOMS_DEV), F32)], 0)
    ext[0:64, 128:384] = feats
    ext[64:72, 128:384] = place
    place4 = turn_rows(place)
    for m in range(NZ):
        rows = feats[8 * m : 8 * m + 8]
        tx1[16 * m : 16 * m + 8] = jnp.where(first4, rows, place4)
        tx1[16 * m + 8 : 16 * m + 16] = jnp.where(first4, turn_rows(rows), place4)
    own = z * NC + core
    rx1[:, 0:ATOMS_DEV] = tx1[pl.ds(pl.multiple_of(own * 8, 8), 8)]

    basis[96:128] = jnp.zeros((32, WIDE), BF16)
    basis[224:256] = jnp.zeros((32, WIDE), BF16)

    pl.semaphore_wait(barrier, len(greeted))

    for r in range(GROUP - 1, 0, -1):
        zz, cc = ring(RING[r])
        group = [g for g, (lo, hi) in enumerate(ARRIVALS) if lo <= r < hi][0]
        send(
            tx1.at[pl.ds(pl.multiple_of((zz * NC + cc) * 8, 8), 8)],
            rx1.at[:, pl.ds(r * ATOMS_DEV, ATOMS_DEV)],
            send_sem.at[0],
            first_sem.at[group],
            at(zz, cc),
        )
    send(ext.at[:, pl.ds(256, 128)], ext.at[:, pl.ds(0, 128)], send_sem.at[1], recv_sem.at[1], upper)
    send(ext.at[:, pl.ds(128, 128)], ext.at[:, pl.ds(384, 128)], send_sem.at[1], recv_sem.at[1], lower)

    m0 = miller_ref[0:1, :]
    code = 9 * miller_ref[1:2, :] + miller_ref[2:3, :]
    code = jnp.where(m0 < 0, -code, code)
    first = jnp.abs(m0)
    pair_at = jnp.abs(code)
    sign = jnp.where(code < 0, -1.0, 1.0)
    kvec = miller_ref.shape[1]
    row128 = rows_like((128, kvec))
    side = jnp.where(row128 < HALF, row128, row128 - HALF)
    hit = (side == pair_at) & (row128 < 2 * HALF)
    plain = jnp.where(hit, 1.0, 0.0)
    signed = jnp.where(hit, jnp.where(row128 < HALF, -sign, sign), 0.0)
    table = jnp.concatenate([plain, signed], 0).astype(BF16)
    channel = 8 * z + 4 * core
    pick = jnp.where(
        lanes_like((8, 64)) == channel + lax.rem(rows_like((8, 64)), 4), 1.0, 0.0
    )
    mine = exact(pick, filter_ref[...], (1, 1))
    upper_rows = rows_like((8, kvec)) // 4
    taken = jnp.concatenate(
        [
            jnp.where(first == 1 + upper_rows, mine, 0.0),
            jnp.where(first == 3 + upper_rows, mine, 0.0),
            jnp.where(first == 0, mine, 0.0),
        ],
        0,
    )
    big = taken.astype(BF16).astype(F32)
    left = taken - big
    middle = left.astype(BF16).astype(F32)
    taken = jnp.concatenate([big, middle, left - middle, jnp.zeros((8, kvec), F32)], 0)
    summed = dot(taken.astype(BF16), table, (1, 1))
    summed = summed[0:24] + summed[24:48] + summed[48:72]
    atoms_all = ATOMS_DEV * lax.axis_size("slab") * lax.axis_size("sub")
    scale = 1.0 / math.sqrt(atoms_all * kvec)
    filters = scale * jnp.concatenate([summed[:, 0:128], summed[0:16, 128:256]], 0)

    energy_row = energy_ref[...]
    energy8 = jnp.sum(pick * energy_row, 1, keepdims=True)
    energy64 = jnp.sum(
        jnp.where(rows_like((64, 64)) == lanes_like((64, 64)), energy_row, 0.0),
        1,
        keepdims=True,
    )

    near = near_ref[...]
    ext_row = rows_like((ATOMS_DEV + 2 * GHOST, ATOMS_DEV))
    count = jnp.zeros(ext_row.shape, F32)
    for n in range(NBR):
        count = count + jnp.where(ext_row == near[n : n + 1, :], 1.0, 0.0)
    pairs[0:64] = jnp.zeros((64, ATOMS_DEV), F32)
    pairs[448:512] = jnp.zeros((64, ATOMS_DEV), F32)
    pairs[64:448] = count

    total = jnp.zeros((80, 256), F32)
    for group, (lo, hi) in enumerate(ARRIVALS):
        width = (hi - lo) * ATOMS_DEV
        here = slice(lo * ATOMS_DEV, hi * ATOMS_DEV)
        recv = rx1.at[:, pl.ds(max(lo, 1) * ATOMS_DEV, (hi - max(lo, 1)) * ATOMS_DEV)]
        wait(recv, first_sem.at[group])
        block = rx1[:, here]
        row = rows_like((88, width))
        pair = jnp.where(row < HALF, row, row - HALF)
        by = (pair + 4) // 9
        cz = (pair - 9 * by).astype(F32)
        shift = jnp.where(row < HALF, 0.0, 0.25)
        turns = by.astype(F32) * block[5:6] + cz * block[6:7] - shift
        waves = jnp.where(row < 2 * HALF, cos_turns(turns), 0.0)
        high, low = halves(waves)
        gap = jnp.zeros((8, width), F32)
        basis[0:96, here] = jnp.concatenate([high, gap], 0).astype(BF16)
        basis[128:224, here] = jnp.concatenate([low, gap], 0).astype(BF16)
        order = (1 + rows_like((8, width)) // 4).astype(F32)
        turns12 = order * block[4:5]
        turns34 = (order + 2.0) * block[4:5]
        waves_x = [
            cos_turns(turns12),
            cos_turns(turns34),
            cos_turns(turns12 - 0.25),
            cos_turns(turns34 - 0.25),
        ]
        for i, wave in enumerate(waves_x):
            xbasis[8 * i : 8 * i + 8, here] = wave
        value = jnp.where(rows_like((8, width)) < 4, block, turn_rows(block))
        feat8[:, here] = value
        modes = jnp.concatenate([value * wave for wave in waves_x] + [value], 0)
        total = total + dot(stacked_halves(modes), basis[:, here], (1, 1))
    own_modes = total[0:40, 0:128] + total[0:40, 128:256] + total[40:80, 0:128]

    def add_y(own_part, src, buf, index, later):
        src[...] = own_part
        for d in range(1, NY):
            send(src, buf.at[d - 1], send_sem.at[index], recv_sem.at[index], along_y(d))
        later()
        wait(buf, recv_sem.at[index])
        out = src[...]
        for d in range(NY - 1):
            out = out + buf[d]
        return out

    def add_x(own_part, src, buf, index, later):
        src[...] = own_part
        for d in range(1, NX):
            send(src, buf.at[d - 1], send_sem.at[index], recv_sem.at[index], along_x(d))
        later()
        wait(buf, recv_sem.at[index])
        out = src[...]
        for d in range(NX - 1):
            out = out + buf[d]
        return out

    def trig_rows(position):
        valid = rows_like(position.shape) < 3
        return jnp.concatenate(
            [
                jnp.where(valid, cos_turns(position), 0.0),
                jnp.where(valid, cos_turns(position - 0.25), 0.0),
            ],
            0,
        )

    def short_values():
        wait(ext.at[:, pl.ds(0, 256)], recv_sem.at[1])
        trig = trig_rows(ext[64:72])
        high, low = halves(trig)
        left_side = jnp.concatenate([high, low, high], 0).astype(BF16)
        right_side = jnp.concatenate([high, high, low], 0)[:, 128:384].astype(BF16)
        closeness = dot(left_side, right_side, (0, 0))
        weights = pairs[...] * jnp.exp(closeness - 3.0)
        pairs[...] = weights
        high, low = halves(weights)
        ext_feat = ext[0:64].astype(BF16)
        short = 0.25 * (dot(ext_feat, high.astype(BF16)) + dot(ext_feat, low.astype(BF16)))
        for m in range(NZ):
            rows = short[8 * m : 8 * m + 8]
            turned = turn_rows(rows)
            tx_short[2 * m] = jnp.where(tile_row < 4, rows[:, 0:128], turned[:, 128:256])
            tx_short[2 * m + 1] = jnp.where(tile_row < 4, turned[:, 0:128], rows[:, 128:256])
        rx_short[0] = tx_short[own]
        for r in range(GROUP - 1, 0, -1):
            zz, cc = ring(RING[r])
            send(
                tx_short.at[zz * NC + cc], rx_short.at[r], send_sem.at[2], recv_sem.at[2], at(zz, cc)
            )

    part = add_y(pack_modes(own_modes), part1, y1, 3, short_values)
    factor = add_x(part, part1x, x1, 4, lambda: None)
    weighted = weigh(factor, filters)
    operand = left_operand(weighted)
    wait(rx_short.at[pl.ds(1, GROUP - 1)], recv_sem.at[2])

    total = jnp.zeros((80, 256), F32)
    blocks = CHUNK // ATOMS_DEV
    for chunk in range(WIDE // CHUNK):
        here = slice(chunk * CHUNK, (chunk + 1) * CHUNK)
        waves_x = [xbasis[8 * i : 8 * i + 8, here] for i in range(4)]
        found = dot(operand, basis[:, here])
        found = found[0:40] + found[40:80]
        field = found[32:40]
        for i in range(4):
            field = field + found[8 * i : 8 * i + 8] * waves_x[i]
        field = field + turn_rows(field)
        pieces = []
        for b in range(blocks):
            tile = rx_short[chunk * blocks + b]
            turned = turn_rows(tile)
            pieces += [
                jnp.where(tile_row < 4, tile, turned),
                jnp.where(tile_row < 4, turned, tile),
            ]
        updated = feat8[:, here] + jnp.concatenate(pieces, 1) + field
        for b in range(blocks):
            tx_upd[chunk * blocks + b] = jnp.where(
                tile_row < 4,
                updated[:, b * 256 : b * 256 + 128],
                updated[:, b * 256 + 128 : b * 256 + 256],
            )
        squashed = jnp.tanh(updated)
        gradient = energy8 * (1.0 - squashed * squashed)
        grad8[:, here] = gradient
        modes = jnp.concatenate([gradient * wave for wave in waves_x] + [gradient], 0)
        total = total + dot(stacked_halves(modes), basis[:, here], (1, 1))
    own_modes = total[0:40, 0:128] + total[0:40, 128:256] + total[40:80, 0:128]

    order12 = (TWO_PI * (1 + rows_like((8, CHUNK)) // 4)).astype(F32)
    order34 = order12 + 2.0 * TWO_PI

    def field_slopes(slope_operand, here):
        c12, c34, s12, s34 = (xbasis[8 * i : 8 * i + 8, here] for i in range(4))
        found = dot(slope_operand, basis[:, here])
        found = found[0:120] + found[120:240]
        t = [found[8 * i : 8 * i + 8] for i in range(15)]
        along = [order12 * (c12 * t[2] - s12 * t[0]) + order34 * (c34 * t[3] - s34 * t[1])]
        for base in (5, 10):
            along.append(
                t[base + 4]
                + c12 * t[base]
                + c34 * t[base + 1]
                + s12 * t[base + 2]
                + s34 * t[base + 3]
            )
        return along

    def first_slopes():
        rx_upd[own] = tx_upd[0]
        for r in range(GROUP - 1, 0, -1):
            zz, cc = ring_back(RING[r])
            send(tx_upd.at[r], rx_upd.at[own], send_sem.at[5], recv_sem.at[5], at(zz, cc))
        slope_operand = left_operand(with_slopes(weighted))
        for chunk in range(WIDE // CHUNK):
            here = slice(chunk * CHUNK, (chunk + 1) * CHUNK)
            gradient = grad8[:, here]
            for d, value in enumerate(field_slopes(slope_operand, here)):
                slopes[8 * d : 8 * d + 8, here] = gradient * value

    short_force = []

    def short_forces():
        others = rx_upd.at[pl.ds(0, GROUP - 1)]
        wait(others, recv_sem.at[5])
        for m in range(NZ):
            low, high = rx_upd[2 * m], rx_upd[2 * m + 1]
            upd_ref[8 * m : 8 * m + 8, 0:128] = jnp.where(tile_row < 4, low, turn_rows(high))
            upd_ref[8 * m : 8 * m + 8, 128:256] = jnp.where(tile_row < 4, turn_rows(low), high)
        squashed = jnp.tanh(upd_ref[...])
        gradient = energy64 * (1.0 - squashed * squashed)
        ext_feat = ext[0:64]
        doubled = jnp.concatenate([ext_feat, ext_feat], 0).astype(BF16)
        touch = dot(doubled, stacked_halves(gradient), (0, 0))
        force = (-0.25 * TWO_PI) * touch * pairs[...]
        high, low = halves(force)
        high, low = high.astype(BF16), low.astype(BF16)
        trig = trig_rows(ext[64:72])
        trig_own = trig[:, 128:384]
        both = stacked_halves(trig)
        found_h, found_l = dot(both, high), dot(both, low)
        found = found_h[0:16] + found_h[16:32] + found_l[0:16]
        mine_acc = trig_own[8:16] * found[0:8] - trig_own[0:8] * found[8:16]
        both = stacked_halves(trig_own)
        found_h, found_l = dot(both, high, (1, 1)), dot(both, low, (1, 1))
        found = found_h[0:16] + found_h[16:32] + found_l[0:16]
        ext_acc = trig[8:16] * found[0:8] - trig[0:8] * found[8:16]
        ghost_out[0] = ext_acc[:, 0:128]
        ghost_out[1] = ext_acc[:, 384:512]
        send(ghost_out.at[0], ghost_in.at[1], send_sem.at[6], recv_sem.at[6], lower)
        send(ghost_out.at[1], ghost_in.at[0], send_sem.at[6], recv_sem.at[6], upper)
        short_force.append(mine_acc + ext_acc[:, 128:384])

    part = add_y(pack_modes(own_modes), part2, y2, 7, first_slopes)
    factor = add_x(part, part2x, x2, 8, short_forces)
    slope_operand = left_operand(with_slopes(weigh(factor, filters)))
    for chunk in range(WIDE // CHUNK):
        here = slice(chunk * CHUNK, (chunk + 1) * CHUNK)
        value = feat8[:, here]
        sums = [
            jnp.sum(slopes[8 * d : 8 * d + 8, here] + value * along, 0, keepdims=True)
            for d, along in enumerate(field_slopes(slope_operand, here))
        ]
        sums = jnp.concatenate(sums + [jnp.zeros((5, CHUNK), F32)], 0)
        for b in range(blocks):
            tx_force[chunk * blocks + b] = jnp.where(
                tile_row < 4,
                sums[:, b * 256 : b * 256 + 128],
                turn_rows(sums[:, b * 256 + 128 : b * 256 + 256]),
            )
    for r in range(GROUP - 1, 0, -1):
        send(
            tx_force.at[r],
            rx_force.at[r - 1],
            send_sem.at[9],
            recv_sem.at[9],
            at(*ring_back(RING[r])),
        )
    wait(ghost_in, recv_sem.at[6])
    rest = short_force[0] + jnp.concatenate([ghost_in[0], ghost_in[1]], 1)
    wait(rx_force, recv_sem.at[9])
    pulled = tx_force[0]
    for r in range(GROUP - 1):
        pulled = pulled + rx_force[r]
    rest = rest + jnp.concatenate([pulled, turn_rows(pulled)], 1)
    force_ref[...] = -rest[0:3]

    wait(tx1.at[pl.ds(0, 8 * (GROUP - 1))], send_sem.at[0])
    wait(ext.at[:, pl.ds(0, 256)], send_sem.at[1])
    wait(tx_short.at[pl.ds(0, GROUP - 1)], send_sem.at[2])
    wait(y1, send_sem.at[3])
    wait(x1, send_sem.at[4])
    wait(tx_upd.at[pl.ds(0, GROUP - 1)], send_sem.at[5])
    wait(ghost_out, send_sem.at[6])
    wait(y2, send_sem.at[7])
    wait(x2, send_sem.at[8])
    wait(tx_force.at[pl.ds(0, GROUP - 1)], send_sem.at[9])


def on_device(positions, features, neighbours, miller, filter_weights, energy_weights):
    vmem = pl.BlockSpec(memory_space=pltpu.VMEM)
    scratch = [
        ((GROUP * 8, ATOMS_DEV), F32),
        ((8, WIDE), F32),
        ((72, 512), F32),
        ((256, WIDE), BF16),
        ((32, WIDE), F32),
        ((8, WIDE), F32),
        ((8, WIDE), F32),
        ((24, WIDE), F32),
        ((512, ATOMS_DEV), F32),
        ((NY - 1, 24, 128), F32),
        ((NX - 1, 24, 128), F32),
        ((NY - 1, 24, 128), F32),
        ((NX - 1, 24, 128), F32),
        ((24, 128), F32),
        ((24, 128), F32),
        ((24, 128), F32),
        ((24, 128), F32),
        ((GROUP, 8, 128), F32),
        ((GROUP, 8, 128), F32),
        ((GROUP, 8, 128), F32),
        ((GROUP, 8, 128), F32),
        ((GROUP, 8, 128), F32),
        ((GROUP - 1, 8, 128), F32),
        ((2, 8, 128), F32),
        ((2, 8, 128), F32),
    ]
    return pl.pallas_call(
        kernel,
        out_shape=(
            jax.ShapeDtypeStruct((64, ATOMS_DEV), F32),
            jax.ShapeDtypeStruct((3, ATOMS_DEV), F32),
        ),
        in_specs=[vmem] * 6,
        out_specs=(vmem, vmem),
        scratch_shapes=[pltpu.VMEM(shape, kind) for shape, kind in scratch]
        + [
            pltpu.SemaphoreType.DMA((len(ARRIVALS),)),
            pltpu.SemaphoreType.DMA((10,)),
            pltpu.SemaphoreType.DMA((10,)),
        ],
        compiler_params=pltpu.CompilerParams(
            collective_id=0, has_side_effects=True, vmem_limit_bytes=40 * 2**20
        ),
    )(positions, features, neighbours, miller, filter_weights, energy_weights.reshape(1, 64))


def solution(mesh):
    split = P(None, ("slab", "sub"))
    return jax.shard_map(
        on_device,
        mesh=mesh,
        in_specs=(split, split, split, P(), P(), P()),
        out_specs=(split, split),
        check_vma=False,
    )
```

```python
import functools
import math

import jax
import jax.numpy as jnp
import numpy as np
from jax import lax
from jax.experimental import pallas as pl
from jax.experimental.pallas import tpu as pltpu
from jax.sharding import PartitionSpec as P

F32 = jnp.float32
BF16 = jnp.bfloat16
MESH = pl.DeviceIdType.MESH
TWO_PI = 2.0 * math.pi

NZ, NY, NX, NC = 8, 8, 4, 2
ATOMS_DEV = 256
GHOST = 64
NBR = 16
HALF = 40
USED = 2 * HALF + 1
GROUP = NZ * NC
WIDE = GROUP * ATOMS_DEV
CHUNK = 1024

RING = sorted(
    [(dz, dc) for dz in range(NZ) for dc in range(NC)],
    key=lambda o: (min(o[0], NZ - o[0]), o[0], o[1]),
)
FAR_Y = (4, 3, 5, 2, 6, 1, 7)
FAR_X = (2, 1, 3)
ARRIVALS = ((0, 2), (2, 6), (6, 10), (10, 14), (14, 16))


def wave_coefficients():
    nodes = np.cos(np.pi * (np.arange(64) + 0.5) / 64)
    square = (nodes + 1) / 32
    angle = np.sqrt(square)
    fit = np.polynomial.chebyshev.Chebyshev.fit(
        square, -np.sin(2 * np.pi * angle) / angle, 5, domain=[0, 1 / 16]
    )
    return [float(v) for v in fit.convert(kind=np.polynomial.Polynomial).coef]


WAVE = wave_coefficients()


def cos_turns(turns):
    beyond = jnp.abs(turns - jnp.round(turns)) - 0.25
    square = beyond * beyond
    value = jnp.full_like(square, WAVE[-1])
    for factor in WAVE[-2::-1]:
        value = value * square + factor
    return value * beyond


def halves(value):
    high = value.astype(BF16).astype(F32)
    return high, value - high


def stacked_halves(value):
    return jnp.concatenate(halves(value), 0).astype(BF16)


def dot(left, right, contract=(1, 0)):
    return lax.dot_general(
        left, right, (((contract[0],), (contract[1],)), ((), ())), preferred_element_type=F32
    )


def exact(left, right, contract=(1, 0)):
    return lax.dot_general(
        left,
        right,
        (((contract[0],), (contract[1],)), ((), ())),
        precision=lax.Precision.HIGHEST,
        preferred_element_type=F32,
    )


def rows_like(shape):
    return lax.broadcasted_iota(jnp.int32, shape, 0)


def lanes_like(shape):
    return lax.broadcasted_iota(jnp.int32, shape, 1)


def turn_rows(value):
    return pltpu.roll(value, 4, 0)


def turn_lanes(value, by):
    return pltpu.roll(value, by % 128, 1)


def swap_sides(value):
    lane = lanes_like(value.shape)
    return jnp.where(lane < HALF, turn_lanes(value, -HALF), turn_lanes(value, HALF))


def pack_modes(modes):
    lane = lanes_like((8, 128))
    row = rows_like((8, 128))
    t0, t1, t2, t3, t4 = (modes[8 * i : 8 * i + 8] for i in range(5))
    used = lane < USED
    rest = USED - HALF
    return jnp.concatenate(
        [
            jnp.where(used, t0, turn_lanes(t3, USED)),
            jnp.where(used, t1, turn_lanes(t3, rest)),
            jnp.where(used, t2, jnp.where(row < 4, turn_lanes(t4, USED), turn_lanes(t4, rest))),
        ],
        0,
    )


def unpack_modes(packed):
    lane = lanes_like((8, 128))
    row = rows_like((8, 128))
    p0, p1, p2 = (packed[8 * i : 8 * i + 8] for i in range(3))
    used = lane < USED
    rest = USED - HALF
    t0, t1, t2 = (jnp.where(used, p, 0.0) for p in (p0, p1, p2))
    t3 = jnp.where(lane < HALF, turn_lanes(p0, -USED), turn_lanes(p1, -rest))
    t4 = jnp.where(lane < HALF, turn_lanes(p2, -USED), turn_lanes(turn_rows(p2), -rest))
    t3 = jnp.where(used, t3, 0.0)
    t4 = jnp.where(used & (row < 4), t4, 0.0)
    return t0, t1, t2, t3, t4


def pair_of(lane):
    last = lane >= HALF - 8
    inside = lane % 8
    b = jnp.where(last, jnp.where(inside < 4, inside + 1, 0), lane // 8 + 1)
    c = jnp.where(last, jnp.where(inside < 4, 4, inside - 3), inside - 4)
    return b, c


def lane_of(code):
    b = sum((code >= 9 * i - 4).astype(jnp.int32) for i in range(1, 5))
    c = code - 9 * b
    inner = jnp.where(c == 4, HALF - 9 + b, 8 * b - 4 + c)
    lane = jnp.where(b == 0, HALF - 5 + code, inner)
    return jnp.where(code == 0, 2 * HALF, lane)


def weigh(packed, filters):
    t0, t1, t2, t3, t4 = unpack_modes(packed)
    sum12, sum34, sum0 = filters[0:8], filters[8:16], filters[16:24]
    dif12, dif34 = filters[24:32], filters[32:40]
    return jnp.concatenate(
        [
            sum12 * t0 + dif12 * swap_sides(t2),
            sum34 * t1 + dif34 * swap_sides(t3),
            sum12 * t2 - dif12 * swap_sides(t0),
            sum34 * t3 - dif34 * swap_sides(t1),
            sum0 * t4,
        ],
        0,
    )


def with_slopes(weighted):
    lane = lanes_like(weighted.shape)
    along_y, along_z = pair_of(jnp.where(lane < HALF, lane, lane - HALF))
    sign = jnp.where(lane < HALF, TWO_PI, -TWO_PI)
    sign = jnp.where(lane < 2 * HALF, sign, 0.0)
    swapped = swap_sides(weighted)
    return jnp.concatenate(
        [
            weighted,
            swapped * (sign * along_y.astype(F32)),
            swapped * (sign * along_z.astype(F32)),
        ],
        0,
    )


def left_operand(modes):
    high, low = halves(modes)
    return jnp.concatenate(
        [
            jnp.concatenate([high, high], 1),
            jnp.concatenate([low, jnp.zeros_like(low)], 1),
        ],
        0,
    ).astype(BF16)


def kernel(
    pos_hbm,
    feat_hbm,
    near_hbm,
    miller_hbm,
    filter_hbm,
    energy_hbm,
    upd_ref,
    force_ref,
    pos_ref,
    feat_ref,
    near_ref,
    miller_ref,
    filter_ref,
    energy_ref,
    tx1,
    rx1,
    ext,
    basis,
    xbasis,
    feat8,
    grad8,
    slopes,
    pairs,
    y1,
    x1,
    y2,
    x2,
    part1,
    part1x,
    part2,
    part2x,
    tx_short,
    rx_short,
    tx_upd,
    rx_upd,
    tx_force,
    rx_force,
    ghost_out,
    ghost_in,
    first_sem,
    recv_sem,
    send_sem,
    load_sem,
):
    slab = lax.axis_index("slab")
    sub = lax.axis_index("sub")
    z = lax.rem(slab, NZ)
    x_lo = slab // NZ
    y = sub // 4
    x_hi = lax.rem(sub // 2, 2)
    core = lax.rem(sub, 2)
    x = x_hi * 2 + x_lo

    def at(zz, cc):
        return {"slab": x_lo * NZ + zz, "sub": y * 4 + x_hi * 2 + cc}

    def ring(off):
        return lax.rem(z + off[0], NZ), lax.rem(core + off[1], NC)

    def ring_back(off):
        return lax.rem(z + NZ - off[0], NZ), lax.rem(core + off[1], NC)

    def along_y(d):
        return {"slab": slab, "sub": lax.rem(y + d, NY) * 4 + x_hi * 2 + core}

    def along_x(d):
        xx = lax.rem(x + d, NX)
        return {"slab": lax.rem(xx, 2) * NZ + z, "sub": y * 4 + (xx // 2) * 2 + core}

    upper = {"slab": lax.rem(slab + 1, 16), "sub": sub}
    lower = {"slab": lax.rem(slab + 15, 16), "sub": sub}

    def send(src, dst, send_at, recv, device):
        pltpu.make_async_remote_copy(
            src_ref=src,
            dst_ref=dst,
            send_sem=send_at,
            recv_sem=recv,
            device_id=device,
            device_id_type=MESH,
        ).start()

    def wait(ref, sem):
        pltpu.make_async_copy(ref, ref, sem).wait()

    loads = [
        pltpu.make_async_copy(src, dst, load_sem.at[i])
        for i, (src, dst) in enumerate(
            [
                (pos_hbm, pos_ref),
                (feat_hbm, feat_ref),
                (miller_hbm, miller_ref),
                (filter_hbm, filter_ref),
                (energy_hbm, energy_ref),
                (near_hbm, near_ref),
            ]
        )
    ]
    for load in loads[:2]:
        load.start()

    barrier = pltpu.get_barrier_semaphore()
    greeted = [at(*ring(off)) for off in RING[:0:-1]]
    greeted += [along_y(d) for d in FAR_Y]
    greeted += [along_x(d) for d in FAR_X]
    greeted += [upper, lower]
    for device in greeted:
        pl.semaphore_signal(barrier, inc=1, device_id=device, device_id_type=MESH)

    for load in loads[2:]:
        load.start()
    basis[96:128] = jnp.zeros((32, WIDE), BF16)
    basis[224:256] = jnp.zeros((32, WIDE), BF16)

    row8 = rows_like((8, ATOMS_DEV))
    tile_row = rows_like((8, 128))
    first4 = row8 < 4

    for load in loads[:2]:
        load.wait()
    feats = feat_ref[...].astype(F32)
    place = jnp.concatenate([pos_ref[...], jnp.zeros((5, ATOMS_DEV), F32)], 0)
    ext[0:64, 128:384] = feats
    ext[64:72, 128:384] = place
    place4 = turn_rows(place)
    for m in range(NZ):
        rows = feats[8 * m : 8 * m + 8]
        tx1[16 * m : 16 * m + 8] = jnp.where(first4, rows, place4)
        tx1[16 * m + 8 : 16 * m + 16] = jnp.where(first4, turn_rows(rows), place4)
    own = z * NC + core
    rx1[:, 0:ATOMS_DEV] = tx1[pl.ds(pl.multiple_of(own * 8, 8), 8)]

    pl.semaphore_wait(barrier, len(greeted))

    for r in range(GROUP - 1, 0, -1):
        zz, cc = ring(RING[r])
        group = [g for g, (lo, hi) in enumerate(ARRIVALS) if lo <= r < hi][0]
        send(
            tx1.at[pl.ds(pl.multiple_of((zz * NC + cc) * 8, 8), 8)],
            rx1.at[:, pl.ds(r * ATOMS_DEV, ATOMS_DEV)],
            send_sem.at[0],
            first_sem.at[group],
            at(zz, cc),
        )
    send(ext.at[:, pl.ds(256, 128)], ext.at[:, pl.ds(0, 128)], send_sem.at[1], recv_sem.at[1], upper)
    send(ext.at[:, pl.ds(128, 128)], ext.at[:, pl.ds(384, 128)], send_sem.at[1], recv_sem.at[1], lower)

    for load in loads[2:]:
        load.wait()
    channel = 8 * z + 4 * core
    pick = jnp.where(
        lanes_like((8, 64)) == channel + lax.rem(rows_like((8, 64)), 4), 1.0, 0.0
    )
    energy_row = energy_ref[...]
    energy8 = jnp.sum(pick * energy_row, 1, keepdims=True)
    energy64 = jnp.sum(
        jnp.where(rows_like((64, 64)) == lanes_like((64, 64)), energy_row, 0.0),
        1,
        keepdims=True,
    )

    near = near_ref[...]
    ext_row = rows_like((ATOMS_DEV + 2 * GHOST, ATOMS_DEV))
    count = jnp.zeros(ext_row.shape, F32)
    for n in range(NBR):
        count = count + jnp.where(ext_row == near[n : n + 1, :], 1.0, 0.0)
    pairs[0:64] = jnp.zeros((64, ATOMS_DEV), F32)
    pairs[448:512] = jnp.zeros((64, ATOMS_DEV), F32)
    pairs[64:448] = count

    total = jnp.zeros((80, 256), F32)
    for group, (lo, hi) in enumerate(ARRIVALS):
        width = (hi - lo) * ATOMS_DEV
        here = slice(lo * ATOMS_DEV, hi * ATOMS_DEV)
        recv = rx1.at[:, pl.ds(max(lo, 1) * ATOMS_DEV, (hi - max(lo, 1)) * ATOMS_DEV)]
        wait(recv, first_sem.at[group])
        block = rx1[:, here]
        row = rows_like((8, width))
        upper_half = row < 4
        place_x, place_y, place_z = (block[i : i + 1] for i in (4, 5, 6))
        quad = (row % 4 + 1).astype(F32)
        turns = quad * jnp.where(upper_half, place_y, place_z)
        cos_yz, sin_yz = cos_turns(turns), cos_turns(turns - 0.25)
        turns = (row - 4).astype(F32) * place_z
        cos_z, sin_z = cos_turns(turns), cos_turns(turns - 0.25)
        cos_tiles, sin_tiles = [], []
        for b in range(4):
            cos_y, sin_y = cos_yz[b : b + 1], sin_yz[b : b + 1]
            cos_tiles.append(cos_y * cos_z - sin_y * sin_z)
            sin_tiles.append(sin_y * cos_z + cos_y * sin_z)
        cos_4z = jnp.where(upper_half, cos_yz[7:8], 1.0)
        sin_4z = jnp.where(upper_half, sin_yz[7:8], 0.0)
        cos_tiles.append(cos_yz * cos_4z - sin_yz * sin_4z)
        sin_tiles.append(sin_yz * cos_4z + cos_yz * sin_4z)
        one = jnp.where(row == 0, 1.0, 0.0)
        high, low = halves(jnp.concatenate(cos_tiles + sin_tiles + [one], 0))
        gap = jnp.zeros((8, width), F32)
        basis[0:96, here] = jnp.concatenate([high, gap], 0).astype(BF16)
        basis[128:224, here] = jnp.concatenate([low, gap], 0).astype(BF16)
        turns = (1 + row // 4).astype(F32) * place_x
        cos_12, sin_12 = cos_turns(turns), cos_turns(turns - 0.25)
        cos_2, sin_2 = cos_12[4:5], sin_12[4:5]
        waves_x = [
            cos_12,
            cos_12 * cos_2 - sin_12 * sin_2,
            sin_12,
            sin_12 * cos_2 + cos_12 * sin_2,
        ]
        for i, wave in enumerate(waves_x):
            xbasis[8 * i : 8 * i + 8, here] = wave
        value = jnp.where(upper_half, block, turn_rows(block))
        feat8[:, here] = value
        modes = jnp.concatenate([value * wave for wave in waves_x] + [value], 0)
        total = total + dot(stacked_halves(modes), basis[:, here], (1, 1))
    own_modes = total[0:40, 0:128] + total[0:40, 128:256] + total[40:80, 0:128]

    def add_y(own_part, src, buf, index, later):
        src[...] = own_part
        for d in FAR_Y:
            send(src, buf.at[d - 1], send_sem.at[index], recv_sem.at[index], along_y(d))
        later()
        wait(buf, recv_sem.at[index])
        out = src[...]
        for d in range(NY - 1):
            out = out + buf[d]
        return out

    def add_x(own_part, src, buf, index, later):
        src[...] = own_part
        for d in FAR_X:
            send(src, buf.at[d - 1], send_sem.at[index], recv_sem.at[index], along_x(d))
        later()
        wait(buf, recv_sem.at[index])
        out = src[...]
        for d in range(NX - 1):
            out = out + buf[d]
        return out

    def trig_rows(position):
        valid = rows_like(position.shape) < 3
        return jnp.concatenate(
            [
                jnp.where(valid, cos_turns(position), 0.0),
                jnp.where(valid, cos_turns(position - 0.25), 0.0),
            ],
            0,
        )

    def short_values():
        wait(ext.at[:, pl.ds(0, 256)], recv_sem.at[1])
        trig = trig_rows(ext[64:72])
        high, low = halves(trig)
        left_side = jnp.concatenate([high, low, high], 0).astype(BF16)
        right_side = jnp.concatenate([high, high, low], 0)[:, 128:384].astype(BF16)
        closeness = dot(left_side, right_side, (0, 0))
        weights = pairs[...] * jnp.exp(closeness - 3.0)
        pairs[...] = weights
        high, low = halves(weights)
        ext_feat = ext[0:64].astype(BF16)
        short = 0.25 * (dot(ext_feat, high.astype(BF16)) + dot(ext_feat, low.astype(BF16)))
        for m in range(NZ):
            rows = short[8 * m : 8 * m + 8]
            turned = turn_rows(rows)
            tx_short[2 * m] = jnp.where(tile_row < 4, rows[:, 0:128], turned[:, 128:256])
            tx_short[2 * m + 1] = jnp.where(tile_row < 4, turned[:, 0:128], rows[:, 128:256])
        rx_short[0] = tx_short[own]
        for r in range(GROUP - 1, 0, -1):
            zz, cc = ring(RING[r])
            send(
                tx_short.at[zz * NC + cc], rx_short.at[r], send_sem.at[2], recv_sem.at[2], at(zz, cc)
            )

    held_filters = []

    def add_filters():
        m0 = miller_ref[0:1, :]
        code = 9 * miller_ref[1:2, :] + miller_ref[2:3, :]
        code = jnp.where(m0 < 0, -code, code)
        first = jnp.abs(m0)
        pair_at = lane_of(jnp.abs(code))
        sign = jnp.where(code < 0, -1.0, 1.0)
        kvec = miller_ref.shape[1]
        row128 = rows_like((128, kvec))
        side = jnp.where((row128 >= HALF) & (row128 < 2 * HALF), row128 - HALF, row128)
        hit = side == pair_at
        plain = jnp.where(hit, 1.0, 0.0)
        signed = jnp.where(hit & (row128 < 2 * HALF), jnp.where(row128 < HALF, -sign, sign), 0.0)
        table = jnp.concatenate([plain, signed], 0).astype(BF16)
        mine = exact(pick, filter_ref[...])
        upper_rows = rows_like((8, kvec)) // 4
        taken = jnp.concatenate(
            [
                jnp.where(first == 1 + upper_rows, mine, 0.0),
                jnp.where(first == 3 + upper_rows, mine, 0.0),
                jnp.where(first == 0, mine, 0.0),
            ],
            0,
        )
        big = taken.astype(BF16).astype(F32)
        left = taken - big
        middle = left.astype(BF16).astype(F32)
        taken = jnp.concatenate([big, middle, left - middle, jnp.zeros((8, kvec), F32)], 0)
        summed = dot(taken.astype(BF16), table, (1, 1))
        summed = summed[0:24] + summed[24:48] + summed[48:72]
        atoms_all = ATOMS_DEV * lax.axis_size("slab") * lax.axis_size("sub")
        scale = 1.0 / math.sqrt(atoms_all * kvec)
        held_filters.append(
            scale * jnp.concatenate([summed[:, 0:128], summed[0:16, 128:256]], 0)
        )

    part = add_y(pack_modes(own_modes), part1, y1, 3, short_values)
    factor = add_x(part, part1x, x1, 4, add_filters)
    filters = held_filters[0]
    weighted = weigh(factor, filters)
    operand = left_operand(weighted)
    wait(rx_short.at[pl.ds(1, GROUP - 1)], recv_sem.at[2])

    total = jnp.zeros((80, 256), F32)
    blocks = CHUNK // ATOMS_DEV
    for chunk in range(WIDE // CHUNK):
        here = slice(chunk * CHUNK, (chunk + 1) * CHUNK)
        waves_x = [xbasis[8 * i : 8 * i + 8, here] for i in range(4)]
        found = dot(operand, basis[:, here])
        found = found[0:40] + found[40:80]
        field = found[32:40]
        for i in range(4):
            field = field + found[8 * i : 8 * i + 8] * waves_x[i]
        field = field + turn_rows(field)
        pieces = []
        for b in range(blocks):
            tile = rx_short[chunk * blocks + b]
            turned = turn_rows(tile)
            pieces += [
                jnp.where(tile_row < 4, tile, turned),
                jnp.where(tile_row < 4, turned, tile),
            ]
        updated = feat8[:, here] + jnp.concatenate(pieces, 1) + field
        for b in range(blocks):
            tx_upd[chunk * blocks + b] = jnp.where(
                tile_row < 4,
                updated[:, b * 256 : b * 256 + 128],
                updated[:, b * 256 + 128 : b * 256 + 256],
            )
        squashed = jnp.tanh(updated)
        gradient = energy8 * (1.0 - squashed * squashed)
        grad8[:, here] = gradient
        modes = jnp.concatenate([gradient * wave for wave in waves_x] + [gradient], 0)
        total = total + dot(stacked_halves(modes), basis[:, here], (1, 1))
    own_modes = total[0:40, 0:128] + total[0:40, 128:256] + total[40:80, 0:128]

    order12 = (TWO_PI * (1 + rows_like((8, CHUNK)) // 4)).astype(F32)
    order34 = order12 + 2.0 * TWO_PI

    def field_slopes(slope_operand, here):
        c12, c34, s12, s34 = (xbasis[8 * i : 8 * i + 8, here] for i in range(4))
        found = dot(slope_operand, basis[:, here])
        found = found[0:120] + found[120:240]
        t = [found[8 * i : 8 * i + 8] for i in range(15)]
        along = [order12 * (c12 * t[2] - s12 * t[0]) + order34 * (c34 * t[3] - s34 * t[1])]
        for base in (5, 10):
            along.append(
                t[base + 4]
                + c12 * t[base]
                + c34 * t[base + 1]
                + s12 * t[base + 2]
                + s34 * t[base + 3]
            )
        return along

    def first_slopes():
        rx_upd[own] = tx_upd[0]
        for r in range(GROUP - 1, 0, -1):
            zz, cc = ring_back(RING[r])
            send(tx_upd.at[r], rx_upd.at[own], send_sem.at[5], recv_sem.at[5], at(zz, cc))
        slope_operand = left_operand(with_slopes(weighted))
        for chunk in range(WIDE // CHUNK):
            here = slice(chunk * CHUNK, (chunk + 1) * CHUNK)
            gradient = grad8[:, here]
            for d, value in enumerate(field_slopes(slope_operand, here)):
                slopes[8 * d : 8 * d + 8, here] = gradient * value

    short_force = []

    def short_forces():
        others = rx_upd.at[pl.ds(0, GROUP - 1)]
        wait(others, recv_sem.at[5])
        for m in range(NZ):
            low, high = rx_upd[2 * m], rx_upd[2 * m + 1]
            upd_ref[8 * m : 8 * m + 8, 0:128] = jnp.where(tile_row < 4, low, turn_rows(high))
            upd_ref[8 * m : 8 * m + 8, 128:256] = jnp.where(tile_row < 4, turn_rows(low), high)
        squashed = jnp.tanh(upd_ref[...])
        gradient = energy64 * (1.0 - squashed * squashed)
        ext_feat = ext[0:64]
        doubled = jnp.concatenate([ext_feat, ext_feat], 0).astype(BF16)
        touch = dot(doubled, stacked_halves(gradient), (0, 0))
        force = (-0.25 * TWO_PI) * touch * pairs[...]
        high, low = halves(force)
        high, low = high.astype(BF16), low.astype(BF16)
        trig = trig_rows(ext[64:72])
        trig_own = trig[:, 128:384]
        both = stacked_halves(trig)
        found_h, found_l = dot(both, high), dot(both, low)
        found = found_h[0:16] + found_h[16:32] + found_l[0:16]
        mine_acc = trig_own[8:16] * found[0:8] - trig_own[0:8] * found[8:16]
        both = stacked_halves(trig_own)
        found_h, found_l = dot(both, high, (1, 1)), dot(both, low, (1, 1))
        found = found_h[0:16] + found_h[16:32] + found_l[0:16]
        ext_acc = trig[8:16] * found[0:8] - trig[0:8] * found[8:16]
        ghost_out[0] = ext_acc[:, 0:128]
        ghost_out[1] = ext_acc[:, 384:512]
        send(ghost_out.at[0], ghost_in.at[1], send_sem.at[6], recv_sem.at[6], lower)
        send(ghost_out.at[1], ghost_in.at[0], send_sem.at[6], recv_sem.at[6], upper)
        short_force.append(mine_acc + ext_acc[:, 128:384])

    part = add_y(pack_modes(own_modes), part2, y2, 7, first_slopes)
    factor = add_x(part, part2x, x2, 8, short_forces)
    slope_operand = left_operand(with_slopes(weigh(factor, filters)))
    for chunk in range(WIDE // CHUNK - 1, -1, -1):
        here = slice(chunk * CHUNK, (chunk + 1) * CHUNK)
        value = feat8[:, here]
        sums = [
            jnp.sum(slopes[8 * d : 8 * d + 8, here] + value * along, 0, keepdims=True)
            for d, along in enumerate(field_slopes(slope_operand, here))
        ]
        sums = jnp.concatenate(sums + [jnp.zeros((5, CHUNK), F32)], 0)
        for b in range(blocks):
            tx_force[chunk * blocks + b] = jnp.where(
                tile_row < 4,
                sums[:, b * 256 : b * 256 + 128],
                turn_rows(sums[:, b * 256 + 128 : b * 256 + 256]),
            )
        for r in range((chunk + 1) * blocks - 1, max(chunk * blocks, 1) - 1, -1):
            send(
                tx_force.at[r],
                rx_force.at[r - 1],
                send_sem.at[9],
                recv_sem.at[9],
                at(*ring_back(RING[r])),
            )
    wait(ghost_in, recv_sem.at[6])
    rest = short_force[0] + jnp.concatenate([ghost_in[0], ghost_in[1]], 1)
    wait(rx_force, recv_sem.at[9])
    pulled = tx_force[0]
    for r in range(GROUP - 1):
        pulled = pulled + rx_force[r]
    rest = rest + jnp.concatenate([pulled, turn_rows(pulled)], 1)
    force_ref[...] = -rest[0:3]

    wait(tx1.at[pl.ds(0, 8 * (GROUP - 1))], send_sem.at[0])
    wait(ext.at[:, pl.ds(0, 256)], send_sem.at[1])
    wait(tx_short.at[pl.ds(0, GROUP - 1)], send_sem.at[2])
    wait(y1, send_sem.at[3])
    wait(x1, send_sem.at[4])
    wait(tx_upd.at[pl.ds(0, GROUP - 1)], send_sem.at[5])
    wait(ghost_out, send_sem.at[6])
    wait(y2, send_sem.at[7])
    wait(x2, send_sem.at[8])
    wait(tx_force.at[pl.ds(0, GROUP - 1)], send_sem.at[9])


def hand_over(upd_ref, force_ref, upd_out, force_out, sem):
    copies = [
        pltpu.make_async_copy(upd_ref, upd_out, sem.at[0]),
        pltpu.make_async_copy(force_ref, force_out, sem.at[1]),
    ]
    for copy in copies:
        copy.start()
    for copy in copies:
        copy.wait()


def on_device(positions, features, neighbours, miller, filter_weights, energy_weights):
    vmem = pl.BlockSpec(memory_space=pltpu.VMEM)
    hbm = pl.BlockSpec(memory_space=pltpu.HBM)
    filters = filter_weights.T
    energy = energy_weights.reshape(1, 64)
    inputs = (positions, features, neighbours, miller, filters, energy)
    scratch = [(value.shape, value.dtype) for value in inputs] + [
        ((GROUP * 8, ATOMS_DEV), F32),
        ((8, WIDE), F32),
        ((72, 512), F32),
        ((256, WIDE), BF16),
        ((32, WIDE), F32),
        ((8, WIDE), F32),
        ((8, WIDE), F32),
        ((24, WIDE), F32),
        ((512, ATOMS_DEV), F32),
        ((NY - 1, 24, 128), F32),
        ((NX - 1, 24, 128), F32),
        ((NY - 1, 24, 128), F32),
        ((NX - 1, 24, 128), F32),
        ((24, 128), F32),
        ((24, 128), F32),
        ((24, 128), F32),
        ((24, 128), F32),
        ((GROUP, 8, 128), F32),
        ((GROUP, 8, 128), F32),
        ((GROUP, 8, 128), F32),
        ((GROUP, 8, 128), F32),
        ((GROUP, 8, 128), F32),
        ((GROUP - 1, 8, 128), F32),
        ((2, 8, 128), F32),
        ((2, 8, 128), F32),
    ]
    found = pl.pallas_call(
        kernel,
        out_shape=(
            jax.ShapeDtypeStruct((64, ATOMS_DEV), F32),
            jax.ShapeDtypeStruct((3, ATOMS_DEV), F32),
        ),
        in_specs=[hbm] * 6,
        out_specs=(vmem, vmem),
        scratch_shapes=[pltpu.VMEM(shape, kind) for shape, kind in scratch]
        + [
            pltpu.SemaphoreType.DMA((len(ARRIVALS),)),
            pltpu.SemaphoreType.DMA((10,)),
            pltpu.SemaphoreType.DMA((10,)),
            pltpu.SemaphoreType.DMA((len(inputs),)),
        ],
        compiler_params=pltpu.CompilerParams(
            collective_id=0, has_side_effects=True, vmem_limit_bytes=60 * 2**20
        ),
    )(*inputs)
    return pl.pallas_call(
        hand_over,
        out_shape=tuple(jax.ShapeDtypeStruct(value.shape, F32) for value in found),
        in_specs=[vmem] * 2,
        out_specs=(hbm, hbm),
        scratch_shapes=[pltpu.SemaphoreType.DMA((2,))],
    )(*found)


def solution(mesh):
    split = P(None, ("slab", "sub"))
    return jax.shard_map(
        on_device,
        mesh=mesh,
        in_specs=(split, split, split, P(), P(), P()),
        out_specs=(split, split),
        check_vma=False,
    )
```

```python
import functools
import math

import jax
import jax.numpy as jnp
import numpy as np
from jax import lax
from jax.experimental import pallas as pl
from jax.experimental.pallas import tpu as pltpu
from jax.sharding import PartitionSpec as P

F32 = jnp.float32
BF16 = jnp.bfloat16
MESH = pl.DeviceIdType.MESH
TWO_PI = 2.0 * math.pi

NZ, NY, NX, NC = 8, 8, 4, 2
ATOMS_DEV = 256
GHOST = 64
NBR = 16
HALF = 40
USED = 2 * HALF + 1
GROUP = NY * NC
WIDE = GROUP * ATOMS_DEV
CHUNK = 1024

RING = sorted(
    [(dy, dc) for dy in range(NY) for dc in range(NC)],
    key=lambda o: (min(o[0], NY - o[0]), o[0], o[1]),
)
FAR_Z = (4, 3, 5, 2, 6, 1, 7)
FAR_X = (2, 1, 3)
ARRIVALS = ((0, 2), (2, 6), (6, 10), (10, 14), (14, 16))


def wave_coefficients():
    nodes = np.cos(np.pi * (np.arange(64) + 0.5) / 64)
    square = (nodes + 1) / 32
    angle = np.sqrt(square)
    fit = np.polynomial.chebyshev.Chebyshev.fit(
        square, -np.sin(2 * np.pi * angle) / angle, 5, domain=[0, 1 / 16]
    )
    return [float(v) for v in fit.convert(kind=np.polynomial.Polynomial).coef]


WAVE = wave_coefficients()


def cos_turns(turns):
    beyond = jnp.abs(turns - jnp.round(turns)) - 0.25
    square = beyond * beyond
    value = jnp.full_like(square, WAVE[-1])
    for factor in WAVE[-2::-1]:
        value = value * square + factor
    return value * beyond


def halves(value):
    high = value.astype(BF16).astype(F32)
    return high, value - high


def stacked_halves(value):
    return jnp.concatenate(halves(value), 0).astype(BF16)


def dot(left, right, contract=(1, 0)):
    return lax.dot_general(
        left, right, (((contract[0],), (contract[1],)), ((), ())), preferred_element_type=F32
    )


def exact(left, right, contract=(1, 0)):
    return lax.dot_general(
        left,
        right,
        (((contract[0],), (contract[1],)), ((), ())),
        precision=lax.Precision.HIGHEST,
        preferred_element_type=F32,
    )


def rows_like(shape):
    return lax.broadcasted_iota(jnp.int32, shape, 0)


def lanes_like(shape):
    return lax.broadcasted_iota(jnp.int32, shape, 1)


def turn_rows(value):
    return pltpu.roll(value, 4, 0)


def turn_lanes(value, by):
    return pltpu.roll(value, by % 128, 1)


def swap_sides(value):
    lane = lanes_like(value.shape)
    return jnp.where(lane < HALF, turn_lanes(value, -HALF), turn_lanes(value, HALF))


def pack_modes(modes):
    lane = lanes_like((8, 128))
    row = rows_like((8, 128))
    t0, t1, t2, t3, t4 = (modes[8 * i : 8 * i + 8] for i in range(5))
    used = lane < USED
    rest = USED - HALF
    return jnp.concatenate(
        [
            jnp.where(used, t0, turn_lanes(t3, USED)),
            jnp.where(used, t1, turn_lanes(t3, rest)),
            jnp.where(used, t2, jnp.where(row < 4, turn_lanes(t4, USED), turn_lanes(t4, rest))),
        ],
        0,
    )


def unpack_modes(packed):
    lane = lanes_like((8, 128))
    row = rows_like((8, 128))
    p0, p1, p2 = (packed[8 * i : 8 * i + 8] for i in range(3))
    used = lane < USED
    rest = USED - HALF
    t0, t1, t2 = (jnp.where(used, p, 0.0) for p in (p0, p1, p2))
    t3 = jnp.where(lane < HALF, turn_lanes(p0, -USED), turn_lanes(p1, -rest))
    t4 = jnp.where(lane < HALF, turn_lanes(p2, -USED), turn_lanes(turn_rows(p2), -rest))
    t3 = jnp.where(used, t3, 0.0)
    t4 = jnp.where(used & (row < 4), t4, 0.0)
    return t0, t1, t2, t3, t4


def pair_of(lane):
    last = lane >= HALF - 8
    inside = lane % 8
    b = jnp.where(last, jnp.where(inside < 4, inside + 1, 0), lane // 8 + 1)
    c = jnp.where(last, jnp.where(inside < 4, 4, inside - 3), inside - 4)
    return b, c


def lane_of(code):
    b = sum((code >= 9 * i - 4).astype(jnp.int32) for i in range(1, 5))
    c = code - 9 * b
    inner = jnp.where(c == 4, HALF - 9 + b, 8 * b - 4 + c)
    lane = jnp.where(b == 0, HALF - 5 + code, inner)
    return jnp.where(code == 0, 2 * HALF, lane)


def weigh(packed, filters):
    t0, t1, t2, t3, t4 = unpack_modes(packed)
    sum12, sum34, sum0 = filters[0:8], filters[8:16], filters[16:24]
    dif12, dif34 = filters[24:32], filters[32:40]
    return jnp.concatenate(
        [
            sum12 * t0 + dif12 * swap_sides(t2),
            sum34 * t1 + dif34 * swap_sides(t3),
            sum12 * t2 - dif12 * swap_sides(t0),
            sum34 * t3 - dif34 * swap_sides(t1),
            sum0 * t4,
        ],
        0,
    )


def with_slopes(weighted):
    lane = lanes_like(weighted.shape)
    along_y, along_z = pair_of(jnp.where(lane < HALF, lane, lane - HALF))
    sign = jnp.where(lane < HALF, TWO_PI, -TWO_PI)
    sign = jnp.where(lane < 2 * HALF, sign, 0.0)
    swapped = swap_sides(weighted)
    return jnp.concatenate(
        [
            weighted,
            swapped * (sign * along_y.astype(F32)),
            swapped * (sign * along_z.astype(F32)),
        ],
        0,
    )


def left_operand(modes):
    high, low = halves(modes)
    return jnp.concatenate(
        [
            jnp.concatenate([high, high], 1),
            jnp.concatenate([low, jnp.zeros_like(low)], 1),
        ],
        0,
    ).astype(BF16)


def kernel(
    pos_hbm,
    feat_hbm,
    near_hbm,
    miller_hbm,
    filter_hbm,
    energy_hbm,
    upd_ref,
    force_ref,
    pos_ref,
    feat_ref,
    near_ref,
    miller_ref,
    filter_ref,
    energy_ref,
    tx1,
    rx1,
    ext,
    basis,
    xbasis,
    feat8,
    grad8,
    slopes,
    pairs,
    z1,
    x1,
    z2,
    x2,
    part1,
    part1x,
    part2,
    part2x,
    tx_short,
    rx_short,
    tx_upd,
    rx_upd,
    tx_force,
    rx_force,
    ghost_out,
    ghost_in,
    first_sem,
    recv_sem,
    send_sem,
    load_sem,
):
    slab = lax.axis_index("slab")
    sub = lax.axis_index("sub")
    z = lax.rem(slab, NZ)
    x_lo = slab // NZ
    y = sub // 4
    x_hi = lax.rem(sub // 2, 2)
    core = lax.rem(sub, 2)
    x = x_hi * 2 + x_lo

    def at(yy, cc):
        return {"slab": slab, "sub": yy * 4 + x_hi * 2 + cc}

    def ring(off):
        return lax.rem(y + off[0], NY), lax.rem(core + off[1], NC)

    def ring_back(off):
        return lax.rem(y + NY - off[0], NY), lax.rem(core + off[1], NC)

    def along_z(d):
        return {"slab": x_lo * NZ + lax.rem(z + d, NZ), "sub": sub}

    def along_x(d):
        xx = lax.rem(x + d, NX)
        return {"slab": lax.rem(xx, 2) * NZ + z, "sub": y * 4 + (xx // 2) * 2 + core}

    upper = {"slab": lax.rem(slab + 1, 16), "sub": sub}
    lower = {"slab": lax.rem(slab + 15, 16), "sub": sub}

    def send(src, dst, send_at, recv, device):
        pltpu.make_async_remote_copy(
            src_ref=src,
            dst_ref=dst,
            send_sem=send_at,
            recv_sem=recv,
            device_id=device,
            device_id_type=MESH,
        ).start()

    def wait(ref, sem):
        pltpu.make_async_copy(ref, ref, sem).wait()

    loads = [
        pltpu.make_async_copy(src, dst, load_sem.at[i])
        for i, (src, dst) in enumerate(
            [
                (pos_hbm, pos_ref),
                (feat_hbm, feat_ref),
                (miller_hbm, miller_ref),
                (filter_hbm, filter_ref),
                (energy_hbm, energy_ref),
                (near_hbm, near_ref),
            ]
        )
    ]
    for load in loads[:2]:
        load.start()

    barrier = pltpu.get_barrier_semaphore()
    greeted = [at(*ring(off)) for off in RING[:0:-1]]
    greeted += [along_z(d) for d in FAR_Z]
    greeted += [along_x(d) for d in FAR_X]
    greeted += [upper, lower]
    for device in greeted:
        pl.semaphore_signal(barrier, inc=1, device_id=device, device_id_type=MESH)

    for load in loads[2:]:
        load.start()
    basis[96:128] = jnp.zeros((32, WIDE), BF16)
    basis[224:256] = jnp.zeros((32, WIDE), BF16)

    row8 = rows_like((8, ATOMS_DEV))
    tile_row = rows_like((8, 128))
    first4 = row8 < 4

    for load in loads[:2]:
        load.wait()
    feats = feat_ref[...].astype(F32)
    place = jnp.concatenate([pos_ref[...], jnp.zeros((5, ATOMS_DEV), F32)], 0)
    ext[0:64, 128:384] = feats
    ext[64:72, 128:384] = place
    place4 = turn_rows(place)
    for m in range(NY):
        rows = feats[8 * m : 8 * m + 8]
        tx1[16 * m : 16 * m + 8] = jnp.where(first4, rows, place4)
        tx1[16 * m + 8 : 16 * m + 16] = jnp.where(first4, turn_rows(rows), place4)
    own = y * NC + core
    rx1[:, 0:ATOMS_DEV] = tx1[pl.ds(pl.multiple_of(own * 8, 8), 8)]

    pl.semaphore_wait(barrier, len(greeted))

    for r in range(GROUP - 1, 0, -1):
        yy, cc = ring(RING[r])
        group = [g for g, (lo, hi) in enumerate(ARRIVALS) if lo <= r < hi][0]
        send(
            tx1.at[pl.ds(pl.multiple_of((yy * NC + cc) * 8, 8), 8)],
            rx1.at[:, pl.ds(r * ATOMS_DEV, ATOMS_DEV)],
            send_sem.at[0],
            first_sem.at[group],
            at(yy, cc),
        )
    send(ext.at[:, pl.ds(256, 128)], ext.at[:, pl.ds(0, 128)], send_sem.at[1], recv_sem.at[1], upper)
    send(ext.at[:, pl.ds(128, 128)], ext.at[:, pl.ds(384, 128)], send_sem.at[1], recv_sem.at[1], lower)

    for load in loads[2:]:
        load.wait()
    channel = 8 * y + 4 * core
    pick = jnp.where(
        lanes_like((8, 64)) == channel + lax.rem(rows_like((8, 64)), 4), 1.0, 0.0
    )
    energy_row = energy_ref[...]
    energy8 = jnp.sum(pick * energy_row, 1, keepdims=True)
    energy64 = jnp.sum(
        jnp.where(rows_like((64, 64)) == lanes_like((64, 64)), energy_row, 0.0),
        1,
        keepdims=True,
    )

    near = near_ref[...]
    ext_row = rows_like((ATOMS_DEV + 2 * GHOST, ATOMS_DEV))
    count = jnp.zeros(ext_row.shape, F32)
    for n in range(NBR):
        count = count + jnp.where(ext_row == near[n : n + 1, :], 1.0, 0.0)
    pairs[0:64] = jnp.zeros((64, ATOMS_DEV), F32)
    pairs[448:512] = jnp.zeros((64, ATOMS_DEV), F32)
    pairs[64:448] = count

    total = jnp.zeros((80, 256), F32)
    for group, (lo, hi) in enumerate(ARRIVALS):
        width = (hi - lo) * ATOMS_DEV
        here = slice(lo * ATOMS_DEV, hi * ATOMS_DEV)
        recv = rx1.at[:, pl.ds(max(lo, 1) * ATOMS_DEV, (hi - max(lo, 1)) * ATOMS_DEV)]
        wait(recv, first_sem.at[group])
        block = rx1[:, here]
        row = rows_like((8, width))
        upper_half = row < 4
        place_x, place_y, place_z = (block[i : i + 1] for i in (4, 5, 6))
        quad = (row % 4 + 1).astype(F32)
        turns = quad * jnp.where(upper_half, place_y, place_z)
        cos_yz, sin_yz = cos_turns(turns), cos_turns(turns - 0.25)
        turns = (row - 4).astype(F32) * place_z
        cos_z, sin_z = cos_turns(turns), cos_turns(turns - 0.25)
        cos_tiles, sin_tiles = [], []
        for b in range(4):
            cos_y, sin_y = cos_yz[b : b + 1], sin_yz[b : b + 1]
            cos_tiles.append(cos_y * cos_z - sin_y * sin_z)
            sin_tiles.append(sin_y * cos_z + cos_y * sin_z)
        cos_4z = jnp.where(upper_half, cos_yz[7:8], 1.0)
        sin_4z = jnp.where(upper_half, sin_yz[7:8], 0.0)
        cos_tiles.append(cos_yz * cos_4z - sin_yz * sin_4z)
        sin_tiles.append(sin_yz * cos_4z + cos_yz * sin_4z)
        one = jnp.where(row == 0, 1.0, 0.0)
        high, low = halves(jnp.concatenate(cos_tiles + sin_tiles + [one], 0))
        gap = jnp.zeros((8, width), F32)
        basis[0:96, here] = jnp.concatenate([high, gap], 0).astype(BF16)
        basis[128:224, here] = jnp.concatenate([low, gap], 0).astype(BF16)
        turns = (1 + row // 4).astype(F32) * place_x
        cos_12, sin_12 = cos_turns(turns), cos_turns(turns - 0.25)
        cos_2, sin_2 = cos_12[4:5], sin_12[4:5]
        waves_x = [
            cos_12,
            cos_12 * cos_2 - sin_12 * sin_2,
            sin_12,
            sin_12 * cos_2 + cos_12 * sin_2,
        ]
        for i, wave in enumerate(waves_x):
            xbasis[8 * i : 8 * i + 8, here] = wave
        value = jnp.where(upper_half, block, turn_rows(block))
        feat8[:, here] = value
        modes = jnp.concatenate([value * wave for wave in waves_x] + [value], 0)
        total = total + dot(stacked_halves(modes), basis[:, here], (1, 1))
    own_modes = total[0:40, 0:128] + total[0:40, 128:256] + total[40:80, 0:128]

    def add_z(own_part, src, buf, index, later):
        src[...] = own_part
        for d in FAR_Z:
            send(src, buf.at[d - 1], send_sem.at[index], recv_sem.at[index], along_z(d))
        later()
        wait(buf, recv_sem.at[index])
        out = src[...]
        for d in range(NZ - 1):
            out = out + buf[d]
        return out

    def add_x(own_part, src, buf, index, later):
        src[...] = own_part
        for d in FAR_X:
            send(src, buf.at[d - 1], send_sem.at[index], recv_sem.at[index], along_x(d))
        later()
        wait(buf, recv_sem.at[index])
        out = src[...]
        for d in range(NX - 1):
            out = out + buf[d]
        return out

    def trig_rows(position):
        valid = rows_like(position.shape) < 3
        return jnp.concatenate(
            [
                jnp.where(valid, cos_turns(position), 0.0),
                jnp.where(valid, cos_turns(position - 0.25), 0.0),
            ],
            0,
        )

    def short_values():
        wait(ext.at[:, pl.ds(0, 256)], recv_sem.at[1])
        trig = trig_rows(ext[64:72])
        high, low = halves(trig)
        left_side = jnp.concatenate([high, low, high], 0).astype(BF16)
        right_side = jnp.concatenate([high, high, low], 0)[:, 128:384].astype(BF16)
        closeness = dot(left_side, right_side, (0, 0))
        weights = pairs[...] * jnp.exp(closeness - 3.0)
        pairs[...] = weights
        high, low = halves(weights)
        ext_feat = ext[0:64].astype(BF16)
        short = 0.25 * (dot(ext_feat, high.astype(BF16)) + dot(ext_feat, low.astype(BF16)))
        for m in range(NY):
            rows = short[8 * m : 8 * m + 8]
            turned = turn_rows(rows)
            tx_short[2 * m] = jnp.where(tile_row < 4, rows[:, 0:128], turned[:, 128:256])
            tx_short[2 * m + 1] = jnp.where(tile_row < 4, turned[:, 0:128], rows[:, 128:256])
        rx_short[0] = tx_short[own]
        for r in range(GROUP - 1, 0, -1):
            yy, cc = ring(RING[r])
            send(
                tx_short.at[yy * NC + cc], rx_short.at[r], send_sem.at[2], recv_sem.at[2], at(yy, cc)
            )

    held_filters = []

    def add_filters():
        m0 = miller_ref[0:1, :]
        code = 9 * miller_ref[1:2, :] + miller_ref[2:3, :]
        code = jnp.where(m0 < 0, -code, code)
        first = jnp.abs(m0)
        pair_at = lane_of(jnp.abs(code))
        sign = jnp.where(code < 0, -1.0, 1.0)
        kvec = miller_ref.shape[1]
        row128 = rows_like((128, kvec))
        side = jnp.where((row128 >= HALF) & (row128 < 2 * HALF), row128 - HALF, row128)
        hit = side == pair_at
        plain = jnp.where(hit, 1.0, 0.0)
        signed = jnp.where(hit & (row128 < 2 * HALF), jnp.where(row128 < HALF, -sign, sign), 0.0)
        table = jnp.concatenate([plain, signed], 0).astype(BF16)
        mine = exact(pick, filter_ref[...])
        upper_rows = rows_like((8, kvec)) // 4
        taken = jnp.concatenate(
            [
                jnp.where(first == 1 + upper_rows, mine, 0.0),
                jnp.where(first == 3 + upper_rows, mine, 0.0),
                jnp.where(first == 0, mine, 0.0),
            ],
            0,
        )
        big = taken.astype(BF16).astype(F32)
        left = taken - big
        middle = left.astype(BF16).astype(F32)
        taken = jnp.concatenate([big, middle, left - middle, jnp.zeros((8, kvec), F32)], 0)
        summed = dot(taken.astype(BF16), table, (1, 1))
        summed = summed[0:24] + summed[24:48] + summed[48:72]
        atoms_all = ATOMS_DEV * lax.axis_size("slab") * lax.axis_size("sub")
        scale = 1.0 / math.sqrt(atoms_all * kvec)
        held_filters.append(
            scale * jnp.concatenate([summed[:, 0:128], summed[0:16, 128:256]], 0)
        )

    part = add_z(pack_modes(own_modes), part1, z1, 3, short_values)
    factor = add_x(part, part1x, x1, 4, add_filters)
    filters = held_filters[0]
    weighted = weigh(factor, filters)
    operand = left_operand(weighted)
    wait(rx_short.at[pl.ds(1, GROUP - 1)], recv_sem.at[2])

    total = jnp.zeros((80, 256), F32)
    blocks = CHUNK // ATOMS_DEV
    for chunk in range(WIDE // CHUNK):
        here = slice(chunk * CHUNK, (chunk + 1) * CHUNK)
        waves_x = [xbasis[8 * i : 8 * i + 8, here] for i in range(4)]
        found = dot(operand, basis[:, here])
        found = found[0:40] + found[40:80]
        field = found[32:40]
        for i in range(4):
            field = field + found[8 * i : 8 * i + 8] * waves_x[i]
        field = field + turn_rows(field)
        pieces = []
        for b in range(blocks):
            tile = rx_short[chunk * blocks + b]
            turned = turn_rows(tile)
            pieces += [
                jnp.where(tile_row < 4, tile, turned),
                jnp.where(tile_row < 4, turned, tile),
            ]
        updated = feat8[:, here] + jnp.concatenate(pieces, 1) + field
        for b in range(blocks):
            tx_upd[chunk * blocks + b] = jnp.where(
                tile_row < 4,
                updated[:, b * 256 : b * 256 + 128],
                updated[:, b * 256 + 128 : b * 256 + 256],
            )
        squashed = jnp.tanh(updated)
        gradient = energy8 * (1.0 - squashed * squashed)
        grad8[:, here] = gradient
        modes = jnp.concatenate([gradient * wave for wave in waves_x] + [gradient], 0)
        total = total + dot(stacked_halves(modes), basis[:, here], (1, 1))
    own_modes = total[0:40, 0:128] + total[0:40, 128:256] + total[40:80, 0:128]

    order12 = (TWO_PI * (1 + rows_like((8, CHUNK)) // 4)).astype(F32)
    order34 = order12 + 2.0 * TWO_PI

    def field_slopes(slope_operand, here):
        c12, c34, s12, s34 = (xbasis[8 * i : 8 * i + 8, here] for i in range(4))
        found = dot(slope_operand, basis[:, here])
        found = found[0:120] + found[120:240]
        t = [found[8 * i : 8 * i + 8] for i in range(15)]
        along = [order12 * (c12 * t[2] - s12 * t[0]) + order34 * (c34 * t[3] - s34 * t[1])]
        for base in (5, 10):
            along.append(
                t[base + 4]
                + c12 * t[base]
                + c34 * t[base + 1]
                + s12 * t[base + 2]
                + s34 * t[base + 3]
            )
        return along

    def first_slopes():
        rx_upd[own] = tx_upd[0]
        for r in range(GROUP - 1, 0, -1):
            yy, cc = ring_back(RING[r])
            send(tx_upd.at[r], rx_upd.at[own], send_sem.at[5], recv_sem.at[5], at(yy, cc))
        slope_operand = left_operand(with_slopes(weighted))
        for chunk in range(WIDE // CHUNK):
            here = slice(chunk * CHUNK, (chunk + 1) * CHUNK)
            gradient = grad8[:, here]
            for d, value in enumerate(field_slopes(slope_operand, here)):
                slopes[8 * d : 8 * d + 8, here] = gradient * value

    short_force = []

    def short_forces():
        others = rx_upd.at[pl.ds(0, GROUP - 1)]
        wait(others, recv_sem.at[5])
        for m in range(NY):
            low, high = rx_upd[2 * m], rx_upd[2 * m + 1]
            upd_ref[8 * m : 8 * m + 8, 0:128] = jnp.where(tile_row < 4, low, turn_rows(high))
            upd_ref[8 * m : 8 * m + 8, 128:256] = jnp.where(tile_row < 4, turn_rows(low), high)
        squashed = jnp.tanh(upd_ref[...])
        gradient = energy64 * (1.0 - squashed * squashed)
        ext_feat = ext[0:64]
        doubled = jnp.concatenate([ext_feat, ext_feat], 0).astype(BF16)
        touch = dot(doubled, stacked_halves(gradient), (0, 0))
        force = (-0.25 * TWO_PI) * touch * pairs[...]
        high, low = halves(force)
        high, low = high.astype(BF16), low.astype(BF16)
        trig = trig_rows(ext[64:72])
        trig_own = trig[:, 128:384]
        both = stacked_halves(trig)
        found_h, found_l = dot(both, high), dot(both, low)
        found = found_h[0:16] + found_h[16:32] + found_l[0:16]
        mine_acc = trig_own[8:16] * found[0:8] - trig_own[0:8] * found[8:16]
        both = stacked_halves(trig_own)
        found_h, found_l = dot(both, high, (1, 1)), dot(both, low, (1, 1))
        found = found_h[0:16] + found_h[16:32] + found_l[0:16]
        ext_acc = trig[8:16] * found[0:8] - trig[0:8] * found[8:16]
        ghost_out[0] = ext_acc[:, 0:128]
        ghost_out[1] = ext_acc[:, 384:512]
        send(ghost_out.at[0], ghost_in.at[1], send_sem.at[6], recv_sem.at[6], lower)
        send(ghost_out.at[1], ghost_in.at[0], send_sem.at[6], recv_sem.at[6], upper)
        short_force.append(mine_acc + ext_acc[:, 128:384])

    part = add_z(pack_modes(own_modes), part2, z2, 7, first_slopes)
    factor = add_x(part, part2x, x2, 8, short_forces)
    slope_operand = left_operand(with_slopes(weigh(factor, filters)))
    for chunk in range(WIDE // CHUNK - 1, -1, -1):
        here = slice(chunk * CHUNK, (chunk + 1) * CHUNK)
        value = feat8[:, here]
        sums = [
            jnp.sum(slopes[8 * d : 8 * d + 8, here] + value * along, 0, keepdims=True)
            for d, along in enumerate(field_slopes(slope_operand, here))
        ]
        sums = jnp.concatenate(sums + [jnp.zeros((5, CHUNK), F32)], 0)
        for b in range(blocks):
            tx_force[chunk * blocks + b] = jnp.where(
                tile_row < 4,
                sums[:, b * 256 : b * 256 + 128],
                turn_rows(sums[:, b * 256 + 128 : b * 256 + 256]),
            )
        for r in range((chunk + 1) * blocks - 1, max(chunk * blocks, 1) - 1, -1):
            send(
                tx_force.at[r],
                rx_force.at[r - 1],
                send_sem.at[9],
                recv_sem.at[9],
                at(*ring_back(RING[r])),
            )
    wait(ghost_in, recv_sem.at[6])
    rest = short_force[0] + jnp.concatenate([ghost_in[0], ghost_in[1]], 1)
    wait(rx_force, recv_sem.at[9])
    pulled = tx_force[0]
    for r in range(GROUP - 1):
        pulled = pulled + rx_force[r]
    rest = rest + jnp.concatenate([pulled, turn_rows(pulled)], 1)
    force_ref[...] = -rest[0:3]

    wait(tx1.at[pl.ds(0, 8 * (GROUP - 1))], send_sem.at[0])
    wait(ext.at[:, pl.ds(0, 256)], send_sem.at[1])
    wait(tx_short.at[pl.ds(0, GROUP - 1)], send_sem.at[2])
    wait(z1, send_sem.at[3])
    wait(x1, send_sem.at[4])
    wait(tx_upd.at[pl.ds(0, GROUP - 1)], send_sem.at[5])
    wait(ghost_out, send_sem.at[6])
    wait(z2, send_sem.at[7])
    wait(x2, send_sem.at[8])
    wait(tx_force.at[pl.ds(0, GROUP - 1)], send_sem.at[9])


def hand_over(upd_ref, force_ref, upd_out, force_out, sem):
    copies = [
        pltpu.make_async_copy(upd_ref, upd_out, sem.at[0]),
        pltpu.make_async_copy(force_ref, force_out, sem.at[1]),
    ]
    for copy in copies:
        copy.start()
    for copy in copies:
        copy.wait()


def on_device(positions, features, neighbours, miller, filter_weights, energy_weights):
    vmem = pl.BlockSpec(memory_space=pltpu.VMEM)
    hbm = pl.BlockSpec(memory_space=pltpu.HBM)
    filters = filter_weights.T
    energy = energy_weights.reshape(1, 64)
    inputs = (positions, features, neighbours, miller, filters, energy)
    scratch = [(value.shape, value.dtype) for value in inputs] + [
        ((GROUP * 8, ATOMS_DEV), F32),
        ((8, WIDE), F32),
        ((72, 512), F32),
        ((256, WIDE), BF16),
        ((32, WIDE), F32),
        ((8, WIDE), F32),
        ((8, WIDE), F32),
        ((24, WIDE), F32),
        ((512, ATOMS_DEV), F32),
        ((NZ - 1, 24, 128), F32),
        ((NX - 1, 24, 128), F32),
        ((NZ - 1, 24, 128), F32),
        ((NX - 1, 24, 128), F32),
        ((24, 128), F32),
        ((24, 128), F32),
        ((24, 128), F32),
        ((24, 128), F32),
        ((GROUP, 8, 128), F32),
        ((GROUP, 8, 128), F32),
        ((GROUP, 8, 128), F32),
        ((GROUP, 8, 128), F32),
        ((GROUP, 8, 128), F32),
        ((GROUP - 1, 8, 128), F32),
        ((2, 8, 128), F32),
        ((2, 8, 128), F32),
    ]
    found = pl.pallas_call(
        kernel,
        out_shape=(
            jax.ShapeDtypeStruct((64, ATOMS_DEV), F32),
            jax.ShapeDtypeStruct((3, ATOMS_DEV), F32),
        ),
        in_specs=[hbm] * 6,
        out_specs=(vmem, vmem),
        scratch_shapes=[pltpu.VMEM(shape, kind) for shape, kind in scratch]
        + [
            pltpu.SemaphoreType.DMA((len(ARRIVALS),)),
            pltpu.SemaphoreType.DMA((10,)),
            pltpu.SemaphoreType.DMA((10,)),
            pltpu.SemaphoreType.DMA((len(inputs),)),
        ],
        compiler_params=pltpu.CompilerParams(
            collective_id=0, has_side_effects=True, vmem_limit_bytes=60 * 2**20
        ),
    )(*inputs)
    return pl.pallas_call(
        hand_over,
        out_shape=tuple(jax.ShapeDtypeStruct(value.shape, F32) for value in found),
        in_specs=[vmem] * 2,
        out_specs=(hbm, hbm),
        scratch_shapes=[pltpu.SemaphoreType.DMA((2,))],
    )(*found)


def solution(mesh):
    split = P(None, ("slab", "sub"))
    return jax.shard_map(
        on_device,
        mesh=mesh,
        in_specs=(split, split, split, P(), P(), P()),
        out_specs=(split, split),
        check_vma=False,
    )
```

```python
import functools
import math

import jax
import jax.numpy as jnp
import numpy as np
from jax import lax
from jax.experimental import pallas as pl
from jax.experimental.pallas import tpu as pltpu
from jax.sharding import PartitionSpec as P

F32 = jnp.float32
BF16 = jnp.bfloat16
MESH = pl.DeviceIdType.MESH
TWO_PI = 2.0 * math.pi

NZ, NY, NX, NC = 8, 8, 4, 2
ATOMS_DEV = 256
GHOST = 64
NBR = 16
HALF = 40
USED = 2 * HALF + 1
GROUP = NY * NC
WIDE = GROUP * ATOMS_DEV
CHUNK = 512
FORCE_CHUNK = 512

RING = sorted(
    [(dy, dc) for dy in range(NY) for dc in range(NC)],
    key=lambda o: (min(o[0], NY - o[0]), o[0], o[1]),
)
FAR_Z = (4, 3, 5, 2, 6, 1, 7)
FAR_X = (2, 1, 3)
ARRIVALS = ((0, 1), (1, 2), (2, 6), (6, 10), (10, 14), (14, 16))


def wave_coefficients():
    nodes = np.cos(np.pi * (np.arange(64) + 0.5) / 64)
    square = (nodes + 1) / 32
    angle = np.sqrt(square)
    fit = np.polynomial.chebyshev.Chebyshev.fit(
        square, -np.sin(2 * np.pi * angle) / angle, 5, domain=[0, 1 / 16]
    )
    return [float(v) for v in fit.convert(kind=np.polynomial.Polynomial).coef]


WAVE = wave_coefficients()


def cos_turns(turns):
    beyond = jnp.abs(turns - jnp.round(turns)) - 0.25
    square = beyond * beyond
    value = jnp.full_like(square, WAVE[-1])
    for factor in WAVE[-2::-1]:
        value = value * square + factor
    return value * beyond


def halves(value):
    high = value.astype(BF16).astype(F32)
    return high, value - high


def stacked_halves(value):
    return jnp.concatenate(halves(value), 0).astype(BF16)


def dot(left, right, contract=(1, 0)):
    return lax.dot_general(
        left, right, (((contract[0],), (contract[1],)), ((), ())), preferred_element_type=F32
    )


def exact(left, right, contract=(1, 0)):
    return lax.dot_general(
        left,
        right,
        (((contract[0],), (contract[1],)), ((), ())),
        precision=lax.Precision.HIGHEST,
        preferred_element_type=F32,
    )


def rows_like(shape):
    return lax.broadcasted_iota(jnp.int32, shape, 0)


def lanes_like(shape):
    return lax.broadcasted_iota(jnp.int32, shape, 1)


def turn_rows(value):
    return pltpu.roll(value, 4, 0)


def turn_lanes(value, by):
    return pltpu.roll(value, by % 128, 1)


def swap_sides(value):
    lane = lanes_like(value.shape)
    return jnp.where(lane < HALF, turn_lanes(value, -HALF), turn_lanes(value, HALF))


def pack_modes(modes):
    lane = lanes_like((8, 128))
    row = rows_like((8, 128))
    t0, t1, t2, t3, t4 = (modes[8 * i : 8 * i + 8] for i in range(5))
    used = lane < USED
    rest = USED - HALF
    return jnp.concatenate(
        [
            jnp.where(used, t0, turn_lanes(t3, USED)),
            jnp.where(used, t1, turn_lanes(t3, rest)),
            jnp.where(used, t2, jnp.where(row < 4, turn_lanes(t4, USED), turn_lanes(t4, rest))),
        ],
        0,
    )


def unpack_modes(packed):
    lane = lanes_like((8, 128))
    row = rows_like((8, 128))
    p0, p1, p2 = (packed[8 * i : 8 * i + 8] for i in range(3))
    used = lane < USED
    rest = USED - HALF
    t0, t1, t2 = (jnp.where(used, p, 0.0) for p in (p0, p1, p2))
    t3 = jnp.where(lane < HALF, turn_lanes(p0, -USED), turn_lanes(p1, -rest))
    t4 = jnp.where(lane < HALF, turn_lanes(p2, -USED), turn_lanes(turn_rows(p2), -rest))
    t3 = jnp.where(used, t3, 0.0)
    t4 = jnp.where(used & (row < 4), t4, 0.0)
    return t0, t1, t2, t3, t4


def pair_of(lane):
    last = lane >= HALF - 8
    inside = lane % 8
    b = jnp.where(last, jnp.where(inside < 4, inside + 1, 0), lane // 8 + 1)
    c = jnp.where(last, jnp.where(inside < 4, 4, inside - 3), inside - 4)
    return b, c


def lane_of(code):
    b = sum((code >= 9 * i - 4).astype(jnp.int32) for i in range(1, 5))
    c = code - 9 * b
    inner = jnp.where(c == 4, HALF - 9 + b, 8 * b - 4 + c)
    lane = jnp.where(b == 0, HALF - 5 + code, inner)
    return jnp.where(code == 0, 2 * HALF, lane)


def weigh(packed, filters):
    t0, t1, t2, t3, t4 = unpack_modes(packed)
    sum12, sum34, sum0 = filters[0:8], filters[8:16], filters[16:24]
    dif12, dif34 = filters[24:32], filters[32:40]
    return jnp.concatenate(
        [
            sum12 * t0 + dif12 * swap_sides(t2),
            sum34 * t1 + dif34 * swap_sides(t3),
            sum12 * t2 - dif12 * swap_sides(t0),
            sum34 * t3 - dif34 * swap_sides(t1),
            sum0 * t4,
        ],
        0,
    )


def with_slopes(weighted):
    lane = lanes_like(weighted.shape)
    along_y, along_z = pair_of(jnp.where(lane < HALF, lane, lane - HALF))
    sign = jnp.where(lane < HALF, TWO_PI, -TWO_PI)
    sign = jnp.where(lane < 2 * HALF, sign, 0.0)
    swapped = swap_sides(weighted)
    return jnp.concatenate(
        [
            weighted,
            swapped * (sign * along_y.astype(F32)),
            swapped * (sign * along_z.astype(F32)),
        ],
        0,
    )


def left_operand(modes):
    high, low = halves(modes)
    return jnp.concatenate(
        [
            jnp.concatenate([high, high], 1),
            jnp.concatenate([low, jnp.zeros_like(low)], 1),
        ],
        0,
    ).astype(BF16)


def kernel(
    pos_hbm,
    feat_hbm,
    near_hbm,
    miller_hbm,
    filter_hbm,
    energy_hbm,
    upd_ref,
    force_ref,
    pos_ref,
    feat_ref,
    near_ref,
    miller_ref,
    filter_ref,
    energy_ref,
    tx1,
    rx1,
    ext,
    basis,
    xbasis,
    feat8,
    grad8,
    slopes,
    pairs,
    z1,
    x1,
    z2,
    x2,
    part1,
    part1x,
    part2,
    part2x,
    tx_short,
    rx_short,
    tx_upd,
    rx_upd,
    tx_force,
    rx_force,
    ghost_out,
    ghost_in,
    first_sem,
    recv_sem,
    send_sem,
    load_sem,
):
    slab = lax.axis_index("slab")
    sub = lax.axis_index("sub")
    z = lax.rem(slab, NZ)
    x_lo = slab // NZ
    y = sub // 4
    x_hi = lax.rem(sub // 2, 2)
    core = lax.rem(sub, 2)
    x = x_hi * 2 + x_lo

    def at(yy, cc):
        return {"slab": slab, "sub": yy * 4 + x_hi * 2 + cc}

    def ring(off):
        return lax.rem(y + off[0], NY), lax.rem(core + off[1], NC)

    def ring_back(off):
        return lax.rem(y + NY - off[0], NY), lax.rem(core + off[1], NC)

    def along_z(d):
        return {"slab": x_lo * NZ + lax.rem(z + d, NZ), "sub": sub}

    def along_x(d):
        xx = lax.rem(x + d, NX)
        return {"slab": lax.rem(xx, 2) * NZ + z, "sub": y * 4 + (xx // 2) * 2 + core}

    upper = {"slab": lax.rem(slab + 1, 16), "sub": sub}
    lower = {"slab": lax.rem(slab + 15, 16), "sub": sub}

    def send(src, dst, send_at, recv, device):
        pltpu.make_async_remote_copy(
            src_ref=src,
            dst_ref=dst,
            send_sem=send_at,
            recv_sem=recv,
            device_id=device,
            device_id_type=MESH,
        ).start()

    def wait(ref, sem):
        pltpu.make_async_copy(ref, ref, sem).wait()

    loads = [
        pltpu.make_async_copy(src, dst, load_sem.at[i])
        for i, (src, dst) in enumerate(
            [
                (pos_hbm, pos_ref),
                (feat_hbm, feat_ref),
                (miller_hbm, miller_ref),
                (filter_hbm, filter_ref),
                (energy_hbm, energy_ref),
                (near_hbm, near_ref),
            ]
        )
    ]
    for load in loads[:2]:
        load.start()

    barrier = pltpu.get_barrier_semaphore()
    greeted = [at(*ring(off)) for off in RING[:0:-1]]
    greeted += [along_z(d) for d in FAR_Z]
    greeted += [along_x(d) for d in FAR_X]
    greeted += [upper, lower]
    for device in greeted:
        pl.semaphore_signal(barrier, inc=1, device_id=device, device_id_type=MESH)

    for load in loads[2:]:
        load.start()
    basis[96:128] = jnp.zeros((32, WIDE), BF16)
    basis[224:256] = jnp.zeros((32, WIDE), BF16)

    row8 = rows_like((8, ATOMS_DEV))
    tile_row = rows_like((8, 128))
    first4 = row8 < 4

    for load in loads[:2]:
        load.wait()
    feats = feat_ref[...].astype(F32)
    place = jnp.concatenate([pos_ref[...], jnp.zeros((5, ATOMS_DEV), F32)], 0)
    ext[0:64, 128:384] = feats
    ext[64:72, 128:384] = place
    place4 = turn_rows(place)
    for m in range(NY):
        rows = feats[8 * m : 8 * m + 8]
        tx1[16 * m : 16 * m + 8] = jnp.where(first4, rows, place4)
        tx1[16 * m + 8 : 16 * m + 16] = jnp.where(first4, turn_rows(rows), place4)
    own = y * NC + core
    rx1[:, 0:ATOMS_DEV] = tx1[pl.ds(pl.multiple_of(own * 8, 8), 8)]

    def block_modes(lo, hi):
        width = (hi - lo) * ATOMS_DEV
        here = slice(lo * ATOMS_DEV, hi * ATOMS_DEV)
        block = rx1[:, here]
        row = rows_like((8, width))
        upper_half = row < 4
        place_x, place_y, place_z = (block[i : i + 1] for i in (4, 5, 6))
        quad = (row % 4 + 1).astype(F32)
        turns = quad * jnp.where(upper_half, place_y, place_z)
        cos_yz, sin_yz = cos_turns(turns), cos_turns(turns - 0.25)
        turns = (row - 4).astype(F32) * place_z
        cos_z, sin_z = cos_turns(turns), cos_turns(turns - 0.25)
        cos_tiles, sin_tiles = [], []
        for b in range(4):
            cos_y, sin_y = cos_yz[b : b + 1], sin_yz[b : b + 1]
            cos_tiles.append(cos_y * cos_z - sin_y * sin_z)
            sin_tiles.append(sin_y * cos_z + cos_y * sin_z)
        cos_4z = jnp.where(upper_half, cos_yz[7:8], 1.0)
        sin_4z = jnp.where(upper_half, sin_yz[7:8], 0.0)
        cos_tiles.append(cos_yz * cos_4z - sin_yz * sin_4z)
        sin_tiles.append(sin_yz * cos_4z + cos_yz * sin_4z)
        one = jnp.where(row == 0, 1.0, 0.0)
        high, low = halves(jnp.concatenate(cos_tiles + sin_tiles + [one], 0))
        gap = jnp.zeros((8, width), F32)
        basis[0:96, here] = jnp.concatenate([high, gap], 0).astype(BF16)
        basis[128:224, here] = jnp.concatenate([low, gap], 0).astype(BF16)
        turns = (1 + row // 4).astype(F32) * place_x
        cos_12, sin_12 = cos_turns(turns), cos_turns(turns - 0.25)
        cos_2, sin_2 = cos_12[4:5], sin_12[4:5]
        waves_x = [
            cos_12,
            cos_12 * cos_2 - sin_12 * sin_2,
            sin_12,
            sin_12 * cos_2 + cos_12 * sin_2,
        ]
        for i, wave in enumerate(waves_x):
            xbasis[8 * i : 8 * i + 8, here] = wave
        value = jnp.where(upper_half, block, turn_rows(block))
        feat8[:, here] = value
        modes = jnp.concatenate([value * wave for wave in waves_x] + [value], 0)
        return dot(stacked_halves(modes), basis[:, here], (1, 1))

    total = block_modes(0, 1)

    loads[5].wait()
    near = near_ref[...]
    ext_row = rows_like((ATOMS_DEV + 2 * GHOST, ATOMS_DEV))
    count = jnp.zeros(ext_row.shape, F32)
    for n in range(NBR):
        count = count + jnp.where(ext_row == near[n : n + 1, :], 1.0, 0.0)
    pairs[0:64] = jnp.zeros((64, ATOMS_DEV), F32)
    pairs[448:512] = jnp.zeros((64, ATOMS_DEV), F32)
    pairs[64:448] = count

    pl.semaphore_wait(barrier, len(greeted))

    for r in range(GROUP - 1, 0, -1):
        yy, cc = ring(RING[r])
        group = [g for g, (lo, hi) in enumerate(ARRIVALS) if lo <= r < hi][0]
        send(
            tx1.at[pl.ds(pl.multiple_of((yy * NC + cc) * 8, 8), 8)],
            rx1.at[:, pl.ds(r * ATOMS_DEV, ATOMS_DEV)],
            send_sem.at[0],
            first_sem.at[group],
            at(yy, cc),
        )
    send(ext.at[:, pl.ds(256, 128)], ext.at[:, pl.ds(0, 128)], send_sem.at[1], recv_sem.at[1], upper)
    send(ext.at[:, pl.ds(128, 128)], ext.at[:, pl.ds(384, 128)], send_sem.at[1], recv_sem.at[1], lower)

    for load in loads[2:5]:
        load.wait()
    channel = 8 * y + 4 * core
    pick = jnp.where(
        lanes_like((8, 64)) == channel + lax.rem(rows_like((8, 64)), 4), 1.0, 0.0
    )
    energy_row = energy_ref[...]
    energy8 = jnp.sum(pick * energy_row, 1, keepdims=True)
    energy64 = jnp.sum(
        jnp.where(rows_like((64, 64)) == lanes_like((64, 64)), energy_row, 0.0),
        1,
        keepdims=True,
    )

    for group, (lo, hi) in enumerate(ARRIVALS):
        if lo == 0:
            continue
        wait(rx1.at[:, pl.ds(lo * ATOMS_DEV, (hi - lo) * ATOMS_DEV)], first_sem.at[group])
        total = total + block_modes(lo, hi)
    own_modes = total[0:40, 0:128] + total[0:40, 128:256] + total[40:80, 0:128]

    def add_z(own_part, src, buf, index, later):
        src[...] = own_part
        for d in FAR_Z:
            send(src, buf.at[d - 1], send_sem.at[index], recv_sem.at[index], along_z(d))
        later()
        wait(buf, recv_sem.at[index])
        out = src[...]
        for d in range(NZ - 1):
            out = out + buf[d]
        return out

    def add_x(own_part, src, buf, index, later):
        src[...] = own_part
        for d in FAR_X:
            send(src, buf.at[d - 1], send_sem.at[index], recv_sem.at[index], along_x(d))
        later()
        wait(buf, recv_sem.at[index])
        out = src[...]
        for d in range(NX - 1):
            out = out + buf[d]
        return out

    def trig_rows(position):
        valid = rows_like(position.shape) < 3
        return jnp.concatenate(
            [
                jnp.where(valid, cos_turns(position), 0.0),
                jnp.where(valid, cos_turns(position - 0.25), 0.0),
            ],
            0,
        )

    def short_values():
        wait(ext.at[:, pl.ds(0, 256)], recv_sem.at[1])
        trig = trig_rows(ext[64:72])
        high, low = halves(trig)
        left_side = jnp.concatenate([high, low, high], 0).astype(BF16)
        right_side = jnp.concatenate([high, high, low], 0)[:, 128:384].astype(BF16)
        closeness = dot(left_side, right_side, (0, 0))
        weights = pairs[...] * jnp.exp(closeness - 3.0)
        pairs[...] = weights
        high, low = halves(weights)
        ext_feat = ext[0:64].astype(BF16)
        short = 0.25 * (dot(ext_feat, high.astype(BF16)) + dot(ext_feat, low.astype(BF16)))
        for m in range(NY):
            rows = short[8 * m : 8 * m + 8]
            turned = turn_rows(rows)
            tx_short[2 * m] = jnp.where(tile_row < 4, rows[:, 0:128], turned[:, 128:256])
            tx_short[2 * m + 1] = jnp.where(tile_row < 4, turned[:, 0:128], rows[:, 128:256])
        rx_short[0] = tx_short[own]
        for r in range(GROUP - 1, 0, -1):
            yy, cc = ring(RING[r])
            send(
                tx_short.at[yy * NC + cc], rx_short.at[r], send_sem.at[2], recv_sem.at[2], at(yy, cc)
            )

    held_filters = []

    def add_filters():
        m0 = miller_ref[0:1, :]
        code = 9 * miller_ref[1:2, :] + miller_ref[2:3, :]
        code = jnp.where(m0 < 0, -code, code)
        first = jnp.abs(m0)
        pair_at = lane_of(jnp.abs(code))
        sign = jnp.where(code < 0, -1.0, 1.0)
        kvec = miller_ref.shape[1]
        row128 = rows_like((128, kvec))
        side = jnp.where((row128 >= HALF) & (row128 < 2 * HALF), row128 - HALF, row128)
        hit = side == pair_at
        plain = jnp.where(hit, 1.0, 0.0)
        signed = jnp.where(hit & (row128 < 2 * HALF), jnp.where(row128 < HALF, -sign, sign), 0.0)
        table = jnp.concatenate([plain, signed], 0).astype(BF16)
        mine = exact(pick, filter_ref[...])
        upper_rows = rows_like((8, kvec)) // 4
        taken = jnp.concatenate(
            [
                jnp.where(first == 1 + upper_rows, mine, 0.0),
                jnp.where(first == 3 + upper_rows, mine, 0.0),
                jnp.where(first == 0, mine, 0.0),
            ],
            0,
        )
        big = taken.astype(BF16).astype(F32)
        left = taken - big
        middle = left.astype(BF16).astype(F32)
        taken = jnp.concatenate([big, middle, left - middle, jnp.zeros((8, kvec), F32)], 0)
        summed = dot(taken.astype(BF16), table, (1, 1))
        summed = summed[0:24] + summed[24:48] + summed[48:72]
        atoms_all = ATOMS_DEV * lax.axis_size("slab") * lax.axis_size("sub")
        scale = 1.0 / math.sqrt(atoms_all * kvec)
        held_filters.append(
            scale * jnp.concatenate([summed[:, 0:128], summed[0:16, 128:256]], 0)
        )

    part = add_z(pack_modes(own_modes), part1, z1, 3, short_values)
    factor = add_x(part, part1x, x1, 4, add_filters)
    filters = held_filters[0]
    weighted = weigh(factor, filters)
    operand = left_operand(weighted)
    wait(rx_short.at[pl.ds(1, GROUP - 1)], recv_sem.at[2])

    total = jnp.zeros((80, 256), F32)
    blocks = CHUNK // ATOMS_DEV
    for chunk in range(WIDE // CHUNK):
        here = slice(chunk * CHUNK, (chunk + 1) * CHUNK)
        waves_x = [xbasis[8 * i : 8 * i + 8, here] for i in range(4)]
        found = dot(operand, basis[:, here])
        found = found[0:40] + found[40:80]
        field = found[32:40]
        for i in range(4):
            field = field + found[8 * i : 8 * i + 8] * waves_x[i]
        field = field + turn_rows(field)
        pieces = []
        for b in range(blocks):
            tile = rx_short[chunk * blocks + b]
            turned = turn_rows(tile)
            pieces += [
                jnp.where(tile_row < 4, tile, turned),
                jnp.where(tile_row < 4, turned, tile),
            ]
        updated = feat8[:, here] + jnp.concatenate(pieces, 1) + field
        for b in range(blocks):
            tx_upd[chunk * blocks + b] = jnp.where(
                tile_row < 4,
                updated[:, b * 256 : b * 256 + 128],
                updated[:, b * 256 + 128 : b * 256 + 256],
            )
        squashed = jnp.tanh(updated)
        gradient = energy8 * (1.0 - squashed * squashed)
        grad8[:, here] = gradient
        modes = jnp.concatenate([gradient * wave for wave in waves_x] + [gradient], 0)
        total = total + dot(stacked_halves(modes), basis[:, here], (1, 1))
    own_modes = total[0:40, 0:128] + total[0:40, 128:256] + total[40:80, 0:128]

    order12 = (TWO_PI * (1 + rows_like((8, 128)) // 4)).astype(F32)[:, 0:1]
    order34 = order12 + 2.0 * TWO_PI

    def field_slopes(slope_operand, here):
        c12, c34, s12, s34 = (xbasis[8 * i : 8 * i + 8, here] for i in range(4))
        found = dot(slope_operand, basis[:, here])
        found = found[0:120] + found[120:240]
        t = [found[8 * i : 8 * i + 8] for i in range(15)]
        along = [order12 * (c12 * t[2] - s12 * t[0]) + order34 * (c34 * t[3] - s34 * t[1])]
        for base in (5, 10):
            along.append(
                t[base + 4]
                + c12 * t[base]
                + c34 * t[base + 1]
                + s12 * t[base + 2]
                + s34 * t[base + 3]
            )
        return along

    def first_slopes():
        rx_upd[own] = tx_upd[0]
        for r in range(GROUP - 1, 0, -1):
            yy, cc = ring_back(RING[r])
            send(tx_upd.at[r], rx_upd.at[own], send_sem.at[5], recv_sem.at[5], at(yy, cc))
        slope_operand = left_operand(with_slopes(weighted))
        for chunk in range(WIDE // CHUNK):
            here = slice(chunk * CHUNK, (chunk + 1) * CHUNK)
            gradient = grad8[:, here]
            for d, value in enumerate(field_slopes(slope_operand, here)):
                slopes[8 * d : 8 * d + 8, here] = gradient * value

    short_force = []

    def short_forces():
        others = rx_upd.at[pl.ds(0, GROUP - 1)]
        wait(others, recv_sem.at[5])
        for m in range(NY):
            low, high = rx_upd[2 * m], rx_upd[2 * m + 1]
            upd_ref[8 * m : 8 * m + 8, 0:128] = jnp.where(tile_row < 4, low, turn_rows(high))
            upd_ref[8 * m : 8 * m + 8, 128:256] = jnp.where(tile_row < 4, turn_rows(low), high)
        squashed = jnp.tanh(upd_ref[...])
        gradient = energy64 * (1.0 - squashed * squashed)
        ext_feat = ext[0:64]
        doubled = jnp.concatenate([ext_feat, ext_feat], 0).astype(BF16)
        touch = dot(doubled, stacked_halves(gradient), (0, 0))
        force = (-0.25 * TWO_PI) * touch * pairs[...]
        high, low = halves(force)
        high, low = high.astype(BF16), low.astype(BF16)
        trig = trig_rows(ext[64:72])
        trig_own = trig[:, 128:384]
        both = stacked_halves(trig)
        found_h, found_l = dot(both, high), dot(both, low)
        found = found_h[0:16] + found_h[16:32] + found_l[0:16]
        mine_acc = trig_own[8:16] * found[0:8] - trig_own[0:8] * found[8:16]
        both = stacked_halves(trig_own)
        found_h, found_l = dot(both, high, (1, 1)), dot(both, low, (1, 1))
        found = found_h[0:16] + found_h[16:32] + found_l[0:16]
        ext_acc = trig[8:16] * found[0:8] - trig[0:8] * found[8:16]
        ghost_out[0] = ext_acc[:, 0:128]
        ghost_out[1] = ext_acc[:, 384:512]
        send(ghost_out.at[0], ghost_in.at[1], send_sem.at[6], recv_sem.at[6], lower)
        send(ghost_out.at[1], ghost_in.at[0], send_sem.at[6], recv_sem.at[6], upper)
        short_force.append(mine_acc + ext_acc[:, 128:384])

    part = add_z(pack_modes(own_modes), part2, z2, 7, first_slopes)
    factor = add_x(part, part2x, x2, 8, short_forces)
    slope_operand = left_operand(with_slopes(weigh(factor, filters)))
    force_blocks = FORCE_CHUNK // ATOMS_DEV
    for chunk in range(WIDE // FORCE_CHUNK - 1, -1, -1):
        here = slice(chunk * FORCE_CHUNK, (chunk + 1) * FORCE_CHUNK)
        value = feat8[:, here]
        sums = [
            jnp.sum(slopes[8 * d : 8 * d + 8, here] + value * along, 0, keepdims=True)
            for d, along in enumerate(field_slopes(slope_operand, here))
        ]
        sums = jnp.concatenate(sums + [jnp.zeros((5, FORCE_CHUNK), F32)], 0)
        for b in range(force_blocks):
            tx_force[chunk * force_blocks + b] = jnp.where(
                tile_row < 4,
                sums[:, b * 256 : b * 256 + 128],
                turn_rows(sums[:, b * 256 + 128 : b * 256 + 256]),
            )
        for r in range((chunk + 1) * force_blocks - 1, max(chunk * force_blocks, 1) - 1, -1):
            send(
                tx_force.at[r],
                rx_force.at[r - 1],
                send_sem.at[9],
                recv_sem.at[9],
                at(*ring_back(RING[r])),
            )
    wait(ghost_in, recv_sem.at[6])
    rest = short_force[0] + jnp.concatenate([ghost_in[0], ghost_in[1]], 1)
    wait(rx_force, recv_sem.at[9])
    pulled = tx_force[0]
    for r in range(GROUP - 1):
        pulled = pulled + rx_force[r]
    rest = rest + jnp.concatenate([pulled, turn_rows(pulled)], 1)
    force_ref[...] = -rest[0:3]

    wait(tx1.at[pl.ds(0, 8 * (GROUP - 1))], send_sem.at[0])
    wait(ext.at[:, pl.ds(0, 256)], send_sem.at[1])
    wait(tx_short.at[pl.ds(0, GROUP - 1)], send_sem.at[2])
    wait(z1, send_sem.at[3])
    wait(x1, send_sem.at[4])
    wait(tx_upd.at[pl.ds(0, GROUP - 1)], send_sem.at[5])
    wait(ghost_out, send_sem.at[6])
    wait(z2, send_sem.at[7])
    wait(x2, send_sem.at[8])
    wait(tx_force.at[pl.ds(0, GROUP - 1)], send_sem.at[9])


def hand_over(upd_ref, force_ref, upd_out, force_out, sem):
    copies = [
        pltpu.make_async_copy(upd_ref, upd_out, sem.at[0]),
        pltpu.make_async_copy(force_ref, force_out, sem.at[1]),
    ]
    for copy in copies:
        copy.start()
    for copy in copies:
        copy.wait()


def on_device(positions, features, neighbours, miller, filter_weights, energy_weights):
    vmem = pl.BlockSpec(memory_space=pltpu.VMEM)
    hbm = pl.BlockSpec(memory_space=pltpu.HBM)
    filters = filter_weights.T
    energy = energy_weights.reshape(1, 64)
    inputs = (positions, features, neighbours, miller, filters, energy)
    scratch = [(value.shape, value.dtype) for value in inputs] + [
        ((GROUP * 8, ATOMS_DEV), F32),
        ((8, WIDE), F32),
        ((72, 512), F32),
        ((256, WIDE), BF16),
        ((32, WIDE), F32),
        ((8, WIDE), F32),
        ((8, WIDE), F32),
        ((24, WIDE), F32),
        ((512, ATOMS_DEV), F32),
        ((NZ - 1, 24, 128), F32),
        ((NX - 1, 24, 128), F32),
        ((NZ - 1, 24, 128), F32),
        ((NX - 1, 24, 128), F32),
        ((24, 128), F32),
        ((24, 128), F32),
        ((24, 128), F32),
        ((24, 128), F32),
        ((GROUP, 8, 128), F32),
        ((GROUP, 8, 128), F32),
        ((GROUP, 8, 128), F32),
        ((GROUP, 8, 128), F32),
        ((GROUP, 8, 128), F32),
        ((GROUP - 1, 8, 128), F32),
        ((2, 8, 128), F32),
        ((2, 8, 128), F32),
    ]
    found = pl.pallas_call(
        kernel,
        out_shape=(
            jax.ShapeDtypeStruct((64, ATOMS_DEV), F32),
            jax.ShapeDtypeStruct((3, ATOMS_DEV), F32),
        ),
        in_specs=[hbm] * 6,
        out_specs=(vmem, vmem),
        scratch_shapes=[pltpu.VMEM(shape, kind) for shape, kind in scratch]
        + [
            pltpu.SemaphoreType.DMA((len(ARRIVALS),)),
            pltpu.SemaphoreType.DMA((10,)),
            pltpu.SemaphoreType.DMA((10,)),
            pltpu.SemaphoreType.DMA((len(inputs),)),
        ],
        compiler_params=pltpu.CompilerParams(
            collective_id=0, has_side_effects=True, vmem_limit_bytes=60 * 2**20
        ),
    )(*inputs)
    return pl.pallas_call(
        hand_over,
        out_shape=tuple(jax.ShapeDtypeStruct(value.shape, F32) for value in found),
        in_specs=[vmem] * 2,
        out_specs=(hbm, hbm),
        scratch_shapes=[pltpu.SemaphoreType.DMA((2,))],
    )(*found)


def solution(mesh):
    split = P(None, ("slab", "sub"))
    return jax.shard_map(
        on_device,
        mesh=mesh,
        in_specs=(split, split, split, P(), P(), P()),
        out_specs=(split, split),
        check_vma=False,
    )
```

```python
import functools
import math

import jax
import jax.numpy as jnp
import numpy as np
from jax import lax
from jax.experimental import pallas as pl
from jax.experimental.pallas import tpu as pltpu
from jax.sharding import PartitionSpec as P

F32 = jnp.float32
BF16 = jnp.bfloat16
MESH = pl.DeviceIdType.MESH
TWO_PI = 2.0 * math.pi

NZ, NY, NX, NC = 8, 8, 4, 2
ATOMS_DEV = 256
GHOST = 64
NBR = 16
HALF = 40
USED = 2 * HALF + 1
GROUP = NY * NC
WIDE = GROUP * ATOMS_DEV
CHUNK = 256
FORCE_CHUNK = 512

RING = sorted(
    [(dy, dc) for dy in range(NY) for dc in range(NC)],
    key=lambda o: (min(o[0], NY - o[0]), o[0], o[1]),
)
FAR_Z = (4, 3, 5, 2, 6, 1, 7)
FAR_X = (2, 1, 3)
ARRIVALS = ((0, 1), (1, 2), (2, 6), (6, 10), (10, 14), (14, 16))


def wave_coefficients():
    nodes = np.cos(np.pi * (np.arange(64) + 0.5) / 64)
    square = (nodes + 1) / 32
    angle = np.sqrt(square)
    fit = np.polynomial.chebyshev.Chebyshev.fit(
        square, -np.sin(2 * np.pi * angle) / angle, 5, domain=[0, 1 / 16]
    )
    return [float(v) for v in fit.convert(kind=np.polynomial.Polynomial).coef]


WAVE = wave_coefficients()


def cos_turns(turns):
    beyond = jnp.abs(turns - jnp.round(turns)) - 0.25
    square = beyond * beyond
    value = jnp.full_like(square, WAVE[-1])
    for factor in WAVE[-2::-1]:
        value = value * square + factor
    return value * beyond


def halves(value):
    high = value.astype(BF16).astype(F32)
    return high, value - high


def stacked_halves(value):
    return jnp.concatenate(halves(value), 0).astype(BF16)


def dot(left, right, contract=(1, 0)):
    return lax.dot_general(
        left, right, (((contract[0],), (contract[1],)), ((), ())), preferred_element_type=F32
    )


def exact(left, right, contract=(1, 0)):
    return lax.dot_general(
        left,
        right,
        (((contract[0],), (contract[1],)), ((), ())),
        precision=lax.Precision.HIGHEST,
        preferred_element_type=F32,
    )


def rows_like(shape):
    return lax.broadcasted_iota(jnp.int32, shape, 0)


def lanes_like(shape):
    return lax.broadcasted_iota(jnp.int32, shape, 1)


def turn_rows(value):
    return pltpu.roll(value, 4, 0)


def turn_lanes(value, by):
    return pltpu.roll(value, by % 128, 1)


def swap_sides(value):
    lane = lanes_like(value.shape)
    return jnp.where(lane < HALF, turn_lanes(value, -HALF), turn_lanes(value, HALF))


def pack_modes(modes):
    lane = lanes_like((8, 128))
    row = rows_like((8, 128))
    t0, t1, t2, t3, t4 = (modes[8 * i : 8 * i + 8] for i in range(5))
    used = lane < USED
    rest = USED - HALF
    return jnp.concatenate(
        [
            jnp.where(used, t0, turn_lanes(t3, USED)),
            jnp.where(used, t1, turn_lanes(t3, rest)),
            jnp.where(used, t2, jnp.where(row < 4, turn_lanes(t4, USED), turn_lanes(t4, rest))),
        ],
        0,
    )


def unpack_modes(packed):
    lane = lanes_like((8, 128))
    row = rows_like((8, 128))
    p0, p1, p2 = (packed[8 * i : 8 * i + 8] for i in range(3))
    used = lane < USED
    rest = USED - HALF
    t0, t1, t2 = (jnp.where(used, p, 0.0) for p in (p0, p1, p2))
    t3 = jnp.where(lane < HALF, turn_lanes(p0, -USED), turn_lanes(p1, -rest))
    t4 = jnp.where(lane < HALF, turn_lanes(p2, -USED), turn_lanes(turn_rows(p2), -rest))
    t3 = jnp.where(used, t3, 0.0)
    t4 = jnp.where(used & (row < 4), t4, 0.0)
    return t0, t1, t2, t3, t4


def pair_of(lane):
    last = lane >= HALF - 8
    inside = lane % 8
    b = jnp.where(last, jnp.where(inside < 4, inside + 1, 0), lane // 8 + 1)
    c = jnp.where(last, jnp.where(inside < 4, 4, inside - 3), inside - 4)
    return b, c


def lane_of(code):
    b = sum((code >= 9 * i - 4).astype(jnp.int32) for i in range(1, 5))
    c = code - 9 * b
    inner = jnp.where(c == 4, HALF - 9 + b, 8 * b - 4 + c)
    lane = jnp.where(b == 0, HALF - 5 + code, inner)
    return jnp.where(code == 0, 2 * HALF, lane)


def weigh(packed, filters):
    t0, t1, t2, t3, t4 = unpack_modes(packed)
    sum12, sum34, sum0 = filters[0:8], filters[8:16], filters[16:24]
    dif12, dif34 = filters[24:32], filters[32:40]
    return jnp.concatenate(
        [
            sum12 * t0 + dif12 * swap_sides(t2),
            sum34 * t1 + dif34 * swap_sides(t3),
            sum12 * t2 - dif12 * swap_sides(t0),
            sum34 * t3 - dif34 * swap_sides(t1),
            sum0 * t4,
        ],
        0,
    )


def with_slopes(weighted):
    lane = lanes_like(weighted.shape)
    along_y, along_z = pair_of(jnp.where(lane < HALF, lane, lane - HALF))
    sign = jnp.where(lane < HALF, TWO_PI, -TWO_PI)
    sign = jnp.where(lane < 2 * HALF, sign, 0.0)
    swapped = swap_sides(weighted)
    return jnp.concatenate(
        [
            weighted,
            swapped * (sign * along_y.astype(F32)),
            swapped * (sign * along_z.astype(F32)),
        ],
        0,
    )


def left_operand(modes):
    high, low = halves(modes)
    return jnp.concatenate(
        [
            jnp.concatenate([high, high], 1),
            jnp.concatenate([low, jnp.zeros_like(low)], 1),
        ],
        0,
    ).astype(BF16)


def kernel(
    pos_hbm,
    feat_hbm,
    near_hbm,
    miller_hbm,
    filter_hbm,
    energy_hbm,
    upd_ref,
    force_ref,
    pos_ref,
    feat_ref,
    near_ref,
    miller_ref,
    filter_ref,
    energy_ref,
    tx1,
    rx1,
    ext,
    basis,
    xbasis,
    feat8,
    grad8,
    slopes,
    pairs,
    z1,
    x1,
    z2,
    x2,
    part1,
    part1x,
    part2,
    part2x,
    tx_short,
    rx_short,
    tx_upd,
    rx_upd,
    tx_force,
    rx_force,
    ghost_out,
    ghost_in,
    first_sem,
    recv_sem,
    send_sem,
    load_sem,
):
    slab = lax.axis_index("slab")
    sub = lax.axis_index("sub")
    z = lax.rem(slab, NZ)
    x_lo = slab // NZ
    y = sub // 4
    x_hi = lax.rem(sub // 2, 2)
    core = lax.rem(sub, 2)
    x = x_hi * 2 + x_lo

    def at(yy, cc):
        return {"slab": slab, "sub": yy * 4 + x_hi * 2 + cc}

    def ring(off):
        return lax.rem(y + off[0], NY), lax.rem(core + off[1], NC)

    def ring_back(off):
        return lax.rem(y + NY - off[0], NY), lax.rem(core + off[1], NC)

    def along_z(d):
        return {"slab": x_lo * NZ + lax.rem(z + d, NZ), "sub": sub}

    def along_x(d):
        xx = lax.rem(x + d, NX)
        return {"slab": lax.rem(xx, 2) * NZ + z, "sub": y * 4 + (xx // 2) * 2 + core}

    upper = {"slab": lax.rem(slab + 1, 16), "sub": sub}
    lower = {"slab": lax.rem(slab + 15, 16), "sub": sub}

    def send(src, dst, send_at, recv, device):
        pltpu.make_async_remote_copy(
            src_ref=src,
            dst_ref=dst,
            send_sem=send_at,
            recv_sem=recv,
            device_id=device,
            device_id_type=MESH,
        ).start()

    def wait(ref, sem):
        pltpu.make_async_copy(ref, ref, sem).wait()

    loads = [
        pltpu.make_async_copy(src, dst, load_sem.at[i])
        for i, (src, dst) in enumerate(
            [
                (pos_hbm, pos_ref),
                (feat_hbm, feat_ref),
                (miller_hbm, miller_ref),
                (filter_hbm, filter_ref),
                (energy_hbm, energy_ref),
                (near_hbm, near_ref),
            ]
        )
    ]
    for load in loads[:2]:
        load.start()

    barrier = pltpu.get_barrier_semaphore()
    greeted = [at(*ring(off)) for off in RING[:0:-1]]
    greeted += [along_z(d) for d in FAR_Z]
    greeted += [along_x(d) for d in FAR_X]
    greeted += [upper, lower]
    for device in greeted:
        pl.semaphore_signal(barrier, inc=1, device_id=device, device_id_type=MESH)

    for load in loads[2:]:
        load.start()
    basis[96:128] = jnp.zeros((32, WIDE), BF16)
    basis[224:256] = jnp.zeros((32, WIDE), BF16)

    row8 = rows_like((8, ATOMS_DEV))
    tile_row = rows_like((8, 128))
    first4 = row8 < 4

    for load in loads[:2]:
        load.wait()
    feats = feat_ref[...].astype(F32)
    place = jnp.concatenate([pos_ref[...], jnp.zeros((5, ATOMS_DEV), F32)], 0)
    ext[0:64, 128:384] = feats
    ext[64:72, 128:384] = place
    place4 = turn_rows(place)
    for m in range(NY):
        rows = feats[8 * m : 8 * m + 8]
        tx1[16 * m : 16 * m + 8] = jnp.where(first4, rows, place4)
        tx1[16 * m + 8 : 16 * m + 16] = jnp.where(first4, turn_rows(rows), place4)
    own = y * NC + core
    rx1[:, 0:ATOMS_DEV] = tx1[pl.ds(pl.multiple_of(own * 8, 8), 8)]

    def block_modes(lo, hi):
        width = (hi - lo) * ATOMS_DEV
        here = slice(lo * ATOMS_DEV, hi * ATOMS_DEV)
        block = rx1[:, here]
        row = rows_like((8, width))
        upper_half = row < 4
        place_x, place_y, place_z = (block[i : i + 1] for i in (4, 5, 6))
        quad = (row % 4 + 1).astype(F32)
        turns = quad * jnp.where(upper_half, place_y, place_z)
        cos_yz, sin_yz = cos_turns(turns), cos_turns(turns - 0.25)
        turns = (row - 4).astype(F32) * place_z
        cos_z, sin_z = cos_turns(turns), cos_turns(turns - 0.25)
        cos_tiles, sin_tiles = [], []
        for b in range(4):
            cos_y, sin_y = cos_yz[b : b + 1], sin_yz[b : b + 1]
            cos_tiles.append(cos_y * cos_z - sin_y * sin_z)
            sin_tiles.append(sin_y * cos_z + cos_y * sin_z)
        cos_4z = jnp.where(upper_half, cos_yz[7:8], 1.0)
        sin_4z = jnp.where(upper_half, sin_yz[7:8], 0.0)
        cos_tiles.append(cos_yz * cos_4z - sin_yz * sin_4z)
        sin_tiles.append(sin_yz * cos_4z + cos_yz * sin_4z)
        one = jnp.where(row == 0, 1.0, 0.0)
        high, low = halves(jnp.concatenate(cos_tiles + sin_tiles + [one], 0))
        gap = jnp.zeros((8, width), F32)
        basis[0:96, here] = jnp.concatenate([high, gap], 0).astype(BF16)
        basis[128:224, here] = jnp.concatenate([low, gap], 0).astype(BF16)
        turns = (1 + row // 4).astype(F32) * place_x
        cos_12, sin_12 = cos_turns(turns), cos_turns(turns - 0.25)
        cos_2, sin_2 = cos_12[4:5], sin_12[4:5]
        waves_x = [
            cos_12,
            cos_12 * cos_2 - sin_12 * sin_2,
            sin_12,
            sin_12 * cos_2 + cos_12 * sin_2,
        ]
        for i, wave in enumerate(waves_x):
            xbasis[8 * i : 8 * i + 8, here] = wave
        value = jnp.where(upper_half, block, turn_rows(block))
        feat8[:, here] = value
        modes = jnp.concatenate([value * wave for wave in waves_x] + [value], 0)
        return dot(stacked_halves(modes), basis[:, here], (1, 1))

    total = block_modes(0, 1)

    loads[5].wait()
    near = near_ref[...]
    ext_row = rows_like((ATOMS_DEV + 2 * GHOST, ATOMS_DEV))
    count = jnp.zeros(ext_row.shape, F32)
    for n in range(NBR):
        count = count + jnp.where(ext_row == near[n : n + 1, :], 1.0, 0.0)
    pairs[0:64] = jnp.zeros((64, ATOMS_DEV), F32)
    pairs[448:512] = jnp.zeros((64, ATOMS_DEV), F32)
    pairs[64:448] = count

    pl.semaphore_wait(barrier, len(greeted))

    for r in range(GROUP - 1, 0, -1):
        yy, cc = ring(RING[r])
        group = [g for g, (lo, hi) in enumerate(ARRIVALS) if lo <= r < hi][0]
        send(
            tx1.at[pl.ds(pl.multiple_of((yy * NC + cc) * 8, 8), 8)],
            rx1.at[:, pl.ds(r * ATOMS_DEV, ATOMS_DEV)],
            send_sem.at[0],
            first_sem.at[group],
            at(yy, cc),
        )
    send(ext.at[:, pl.ds(256, 128)], ext.at[:, pl.ds(0, 128)], send_sem.at[1], recv_sem.at[1], upper)
    send(ext.at[:, pl.ds(128, 128)], ext.at[:, pl.ds(384, 128)], send_sem.at[1], recv_sem.at[1], lower)

    for load in loads[2:5]:
        load.wait()
    channel = 8 * y + 4 * core
    pick = jnp.where(
        lanes_like((8, 64)) == channel + lax.rem(rows_like((8, 64)), 4), 1.0, 0.0
    )
    energy_row = energy_ref[...]
    energy8 = jnp.sum(pick * energy_row, 1, keepdims=True)
    energy64 = jnp.sum(
        jnp.where(rows_like((64, 64)) == lanes_like((64, 64)), energy_row, 0.0),
        1,
        keepdims=True,
    )

    for group, (lo, hi) in enumerate(ARRIVALS):
        if lo == 0:
            continue
        wait(rx1.at[:, pl.ds(lo * ATOMS_DEV, (hi - lo) * ATOMS_DEV)], first_sem.at[group])
        total = total + block_modes(lo, hi)
    own_modes = total[0:40, 0:128] + total[0:40, 128:256] + total[40:80, 0:128]

    def add_z(own_part, src, buf, index, later):
        src[...] = own_part
        for d in FAR_Z:
            send(src, buf.at[d - 1], send_sem.at[index], recv_sem.at[index], along_z(d))
        later()
        wait(buf, recv_sem.at[index])
        out = src[...]
        for d in range(NZ - 1):
            out = out + buf[d]
        return out

    def add_x(own_part, src, buf, index, later):
        src[...] = own_part
        for d in FAR_X:
            send(src, buf.at[d - 1], send_sem.at[index], recv_sem.at[index], along_x(d))
        later()
        wait(buf, recv_sem.at[index])
        out = src[...]
        for d in range(NX - 1):
            out = out + buf[d]
        return out

    def trig_rows(position):
        valid = rows_like(position.shape) < 3
        return jnp.concatenate(
            [
                jnp.where(valid, cos_turns(position), 0.0),
                jnp.where(valid, cos_turns(position - 0.25), 0.0),
            ],
            0,
        )

    def short_values():
        wait(ext.at[:, pl.ds(0, 256)], recv_sem.at[1])
        trig = trig_rows(ext[64:72])
        high, low = halves(trig)
        left_side = jnp.concatenate([high, low, high], 0).astype(BF16)
        right_side = jnp.concatenate([high, high, low], 0)[:, 128:384].astype(BF16)
        closeness = dot(left_side, right_side, (0, 0))
        weights = pairs[...] * jnp.exp(closeness - 3.0)
        pairs[...] = weights
        high, low = halves(weights)
        ext_feat = ext[0:64].astype(BF16)
        short = 0.25 * (dot(ext_feat, high.astype(BF16)) + dot(ext_feat, low.astype(BF16)))
        for m in range(NY):
            rows = short[8 * m : 8 * m + 8]
            turned = turn_rows(rows)
            tx_short[2 * m] = jnp.where(tile_row < 4, rows[:, 0:128], turned[:, 128:256])
            tx_short[2 * m + 1] = jnp.where(tile_row < 4, turned[:, 0:128], rows[:, 128:256])
        rx_short[0] = tx_short[own]
        for r in range(GROUP - 1, 0, -1):
            yy, cc = ring(RING[r])
            send(
                tx_short.at[yy * NC + cc], rx_short.at[r], send_sem.at[2], recv_sem.at[2], at(yy, cc)
            )

    held_filters = []

    def add_filters():
        m0 = miller_ref[0:1, :]
        code = 9 * miller_ref[1:2, :] + miller_ref[2:3, :]
        code = jnp.where(m0 < 0, -code, code)
        first = jnp.abs(m0)
        pair_at = lane_of(jnp.abs(code))
        sign = jnp.where(code < 0, -1.0, 1.0)
        kvec = miller_ref.shape[1]
        row128 = rows_like((128, kvec))
        side = jnp.where((row128 >= HALF) & (row128 < 2 * HALF), row128 - HALF, row128)
        hit = side == pair_at
        plain = jnp.where(hit, 1.0, 0.0)
        signed = jnp.where(hit & (row128 < 2 * HALF), jnp.where(row128 < HALF, -sign, sign), 0.0)
        table = jnp.concatenate([plain, signed], 0).astype(BF16)
        mine = exact(pick, filter_ref[...])
        upper_rows = rows_like((8, kvec)) // 4
        taken = jnp.concatenate(
            [
                jnp.where(first == 1 + upper_rows, mine, 0.0),
                jnp.where(first == 3 + upper_rows, mine, 0.0),
                jnp.where(first == 0, mine, 0.0),
            ],
            0,
        )
        big = taken.astype(BF16).astype(F32)
        left = taken - big
        middle = left.astype(BF16).astype(F32)
        taken = jnp.concatenate([big, middle, left - middle, jnp.zeros((8, kvec), F32)], 0)
        summed = dot(taken.astype(BF16), table, (1, 1))
        summed = summed[0:24] + summed[24:48] + summed[48:72]
        atoms_all = ATOMS_DEV * lax.axis_size("slab") * lax.axis_size("sub")
        scale = 1.0 / math.sqrt(atoms_all * kvec)
        held_filters.append(
            scale * jnp.concatenate([summed[:, 0:128], summed[0:16, 128:256]], 0)
        )

    part = add_z(pack_modes(own_modes), part1, z1, 3, short_values)
    factor = add_x(part, part1x, x1, 4, add_filters)
    filters = held_filters[0]
    weighted = weigh(factor, filters)
    operand = left_operand(weighted)
    wait(rx_short.at[pl.ds(1, GROUP - 1)], recv_sem.at[2])

    total = jnp.zeros((80, 256), F32)
    blocks = CHUNK // ATOMS_DEV
    for chunk in range(WIDE // CHUNK):
        here = slice(chunk * CHUNK, (chunk + 1) * CHUNK)
        waves_x = [xbasis[8 * i : 8 * i + 8, here] for i in range(4)]
        found = dot(operand, basis[:, here])
        found = found[0:40] + found[40:80]
        field = found[32:40]
        for i in range(4):
            field = field + found[8 * i : 8 * i + 8] * waves_x[i]
        field = field + turn_rows(field)
        pieces = []
        for b in range(blocks):
            tile = rx_short[chunk * blocks + b]
            turned = turn_rows(tile)
            pieces += [
                jnp.where(tile_row < 4, tile, turned),
                jnp.where(tile_row < 4, turned, tile),
            ]
        updated = feat8[:, here] + jnp.concatenate(pieces, 1) + field
        for b in range(blocks):
            tx_upd[chunk * blocks + b] = jnp.where(
                tile_row < 4,
                updated[:, b * 256 : b * 256 + 128],
                updated[:, b * 256 + 128 : b * 256 + 256],
            )
        squashed = jnp.tanh(updated)
        gradient = energy8 * (1.0 - squashed * squashed)
        grad8[:, here] = gradient
        modes = jnp.concatenate([gradient * wave for wave in waves_x] + [gradient], 0)
        total = total + dot(stacked_halves(modes), basis[:, here], (1, 1))
    own_modes = total[0:40, 0:128] + total[0:40, 128:256] + total[40:80, 0:128]

    order12 = (TWO_PI * (1 + rows_like((8, 128)) // 4)).astype(F32)[:, 0:1]
    order34 = order12 + 2.0 * TWO_PI

    def field_slopes(slope_operand, here):
        c12, c34, s12, s34 = (xbasis[8 * i : 8 * i + 8, here] for i in range(4))
        found = dot(slope_operand, basis[:, here])
        found = found[0:120] + found[120:240]
        t = [found[8 * i : 8 * i + 8] for i in range(15)]
        along = [order12 * (c12 * t[2] - s12 * t[0]) + order34 * (c34 * t[3] - s34 * t[1])]
        for base in (5, 10):
            along.append(
                t[base + 4]
                + c12 * t[base]
                + c34 * t[base + 1]
                + s12 * t[base + 2]
                + s34 * t[base + 3]
            )
        return along

    def first_slopes():
        rx_upd[own] = tx_upd[0]
        for r in range(GROUP - 1, 0, -1):
            yy, cc = ring_back(RING[r])
            send(tx_upd.at[r], rx_upd.at[own], send_sem.at[5], recv_sem.at[5], at(yy, cc))
        slope_operand = left_operand(with_slopes(weighted))
        for chunk in range(WIDE // CHUNK):
            here = slice(chunk * CHUNK, (chunk + 1) * CHUNK)
            gradient = grad8[:, here]
            for d, value in enumerate(field_slopes(slope_operand, here)):
                slopes[8 * d : 8 * d + 8, here] = gradient * value

    short_force = []

    def short_forces():
        others = rx_upd.at[pl.ds(0, GROUP - 1)]
        wait(others, recv_sem.at[5])
        for m in range(NY):
            low, high = rx_upd[2 * m], rx_upd[2 * m + 1]
            upd_ref[8 * m : 8 * m + 8, 0:128] = jnp.where(tile_row < 4, low, turn_rows(high))
            upd_ref[8 * m : 8 * m + 8, 128:256] = jnp.where(tile_row < 4, turn_rows(low), high)
        squashed = jnp.tanh(upd_ref[...])
        gradient = energy64 * (1.0 - squashed * squashed)
        ext_feat = ext[0:64]
        doubled = jnp.concatenate([ext_feat, ext_feat], 0).astype(BF16)
        touch = dot(doubled, stacked_halves(gradient), (0, 0))
        force = (-0.25 * TWO_PI) * touch * pairs[...]
        high, low = halves(force)
        high, low = high.astype(BF16), low.astype(BF16)
        trig = trig_rows(ext[64:72])
        trig_own = trig[:, 128:384]
        both = stacked_halves(trig)
        found_h, found_l = dot(both, high), dot(both, low)
        found = found_h[0:16] + found_h[16:32] + found_l[0:16]
        mine_acc = trig_own[8:16] * found[0:8] - trig_own[0:8] * found[8:16]
        both = stacked_halves(trig_own)
        found_h, found_l = dot(both, high, (1, 1)), dot(both, low, (1, 1))
        found = found_h[0:16] + found_h[16:32] + found_l[0:16]
        ext_acc = trig[8:16] * found[0:8] - trig[0:8] * found[8:16]
        ghost_out[0] = ext_acc[:, 0:128]
        ghost_out[1] = ext_acc[:, 384:512]
        send(ghost_out.at[0], ghost_in.at[1], send_sem.at[6], recv_sem.at[6], lower)
        send(ghost_out.at[1], ghost_in.at[0], send_sem.at[6], recv_sem.at[6], upper)
        short_force.append(mine_acc + ext_acc[:, 128:384])

    part = add_z(pack_modes(own_modes), part2, z2, 7, first_slopes)
    factor = add_x(part, part2x, x2, 8, short_forces)
    slope_operand = left_operand(with_slopes(weigh(factor, filters)))
    force_blocks = FORCE_CHUNK // ATOMS_DEV
    for chunk in range(WIDE // FORCE_CHUNK - 1, -1, -1):
        here = slice(chunk * FORCE_CHUNK, (chunk + 1) * FORCE_CHUNK)
        value = feat8[:, here]
        sums = [
            jnp.sum(slopes[8 * d : 8 * d + 8, here] + value * along, 0, keepdims=True)
            for d, along in enumerate(field_slopes(slope_operand, here))
        ]
        sums = jnp.concatenate(sums + [jnp.zeros((5, FORCE_CHUNK), F32)], 0)
        for b in range(force_blocks):
            tx_force[chunk * force_blocks + b] = jnp.where(
                tile_row < 4,
                sums[:, b * 256 : b * 256 + 128],
                turn_rows(sums[:, b * 256 + 128 : b * 256 + 256]),
            )
        for r in range((chunk + 1) * force_blocks - 1, max(chunk * force_blocks, 1) - 1, -1):
            send(
                tx_force.at[r],
                rx_force.at[r - 1],
                send_sem.at[9],
                recv_sem.at[9],
                at(*ring_back(RING[r])),
            )
    wait(ghost_in, recv_sem.at[6])
    rest = short_force[0] + jnp.concatenate([ghost_in[0], ghost_in[1]], 1)
    wait(rx_force, recv_sem.at[9])
    pulled = tx_force[0]
    for r in range(GROUP - 1):
        pulled = pulled + rx_force[r]
    rest = rest + jnp.concatenate([pulled, turn_rows(pulled)], 1)
    force_ref[...] = -rest[0:3]

    wait(tx1.at[pl.ds(0, 8 * (GROUP - 1))], send_sem.at[0])
    wait(ext.at[:, pl.ds(0, 256)], send_sem.at[1])
    wait(tx_short.at[pl.ds(0, GROUP - 1)], send_sem.at[2])
    wait(z1, send_sem.at[3])
    wait(x1, send_sem.at[4])
    wait(tx_upd.at[pl.ds(0, GROUP - 1)], send_sem.at[5])
    wait(ghost_out, send_sem.at[6])
    wait(z2, send_sem.at[7])
    wait(x2, send_sem.at[8])
    wait(tx_force.at[pl.ds(0, GROUP - 1)], send_sem.at[9])


def hand_over(upd_ref, force_ref, upd_out, force_out, sem):
    copies = [
        pltpu.make_async_copy(upd_ref, upd_out, sem.at[0]),
        pltpu.make_async_copy(force_ref, force_out, sem.at[1]),
    ]
    for copy in copies:
        copy.start()
    for copy in copies:
        copy.wait()


def on_device(positions, features, neighbours, miller, filter_weights, energy_weights):
    vmem = pl.BlockSpec(memory_space=pltpu.VMEM)
    hbm = pl.BlockSpec(memory_space=pltpu.HBM)
    filters = filter_weights.T
    energy = energy_weights.reshape(1, 64)
    inputs = (positions, features, neighbours, miller, filters, energy)
    scratch = [(value.shape, value.dtype) for value in inputs] + [
        ((GROUP * 8, ATOMS_DEV), F32),
        ((8, WIDE), F32),
        ((72, 512), F32),
        ((256, WIDE), BF16),
        ((32, WIDE), F32),
        ((8, WIDE), F32),
        ((8, WIDE), F32),
        ((24, WIDE), F32),
        ((512, ATOMS_DEV), F32),
        ((NZ - 1, 24, 128), F32),
        ((NX - 1, 24, 128), F32),
        ((NZ - 1, 24, 128), F32),
        ((NX - 1, 24, 128), F32),
        ((24, 128), F32),
        ((24, 128), F32),
        ((24, 128), F32),
        ((24, 128), F32),
        ((GROUP, 8, 128), F32),
        ((GROUP, 8, 128), F32),
        ((GROUP, 8, 128), F32),
        ((GROUP, 8, 128), F32),
        ((GROUP, 8, 128), F32),
        ((GROUP - 1, 8, 128), F32),
        ((2, 8, 128), F32),
        ((2, 8, 128), F32),
    ]
    found = pl.pallas_call(
        kernel,
        out_shape=(
            jax.ShapeDtypeStruct((64, ATOMS_DEV), F32),
            jax.ShapeDtypeStruct((3, ATOMS_DEV), F32),
        ),
        in_specs=[hbm] * 6,
        out_specs=(vmem, vmem),
        scratch_shapes=[pltpu.VMEM(shape, kind) for shape, kind in scratch]
        + [
            pltpu.SemaphoreType.DMA((len(ARRIVALS),)),
            pltpu.SemaphoreType.DMA((10,)),
            pltpu.SemaphoreType.DMA((10,)),
            pltpu.SemaphoreType.DMA((len(inputs),)),
        ],
        compiler_params=pltpu.CompilerParams(
            collective_id=0, has_side_effects=True, vmem_limit_bytes=60 * 2**20
        ),
    )(*inputs)
    return pl.pallas_call(
        hand_over,
        out_shape=tuple(jax.ShapeDtypeStruct(value.shape, F32) for value in found),
        in_specs=[vmem] * 2,
        out_specs=(hbm, hbm),
        scratch_shapes=[pltpu.SemaphoreType.DMA((2,))],
    )(*found)


def solution(mesh):
    split = P(None, ("slab", "sub"))
    return jax.shard_map(
        on_device,
        mesh=mesh,
        in_specs=(split, split, split, P(), P(), P()),
        out_specs=(split, split),
        check_vma=False,
    )
```
